256 devices in a mesh: dp: 4 (over y), expert: 64 (over x, z, core).
Axes of the slice: x: 4, y: 4, z: 8, core: 2. Of those that a mesh axis runs over, the one named last changes fastest.
Arguments:
- tokens: bfloat16 [16384, 2048], P(('dp', 'expert')), may hold values from -6 to 6
- expert_ids: int32 [16384, 8], P(('dp', 'expert')), may hold values from 0 to 63, as said below
- gate_numer: int32 [16384, 8], P(('dp', 'expert')), may hold values from 1 to 64
- w_gate: bfloat16 [64, 2048, 384], P('expert'), may hold values from -0.125 to 0.125
- w_up: bfloat16 [64, 2048, 384], P('expert'), may hold values from -0.125 to 0.125
- w_down: bfloat16 [64, 384, 2048], P('expert'), may hold values from -0.3125 to 0.3125
- shared_gate: bfloat16 [2048, 384], replicated, may hold values from -0.125 to 0.125
- shared_up: bfloat16 [2048, 384], replicated, may hold values from -0.125 to 0.125
- shared_down: bfloat16 [384, 2048], replicated, may hold values from -0.3125 to 0.3125
- d_out: bfloat16 [16384, 2048], P(('dp', 'expert')), may hold values from -6 to 6
Outputs:
- mixed: bfloat16 [16384, 2048], P(('dp', 'expert'))
- d_tokens: bfloat16 [16384, 2048], P(('dp', 'expert'))
- grad_gate: float32 [64, 2048, 384], P('expert', 'dp')
- grad_up: float32 [64, 2048, 384], P('expert', 'dp')
- grad_down: float32 [64, 384, 2048], P('expert', None, 'dp')
The draws below stay inside these ranges and needn't reach their ends.
Inputs may be any that keep to these rules, and one draw needn't show every extreme that they name: `expert_ids`: each token names 8 different experts, two from each of 4 of the 8 groups of consecutive experts. The tokens of one device name one expert 11 times at most, and in every draw some experts are named exactly 11 times by the tokens of every device.
All inputs are finite; a program needn't handle non-finite values.
Results may differ from the reference program's by a relative error of at most 0.012.
Values may be sent and summed in bfloat16 or wider, within the bound.
No kernel may reach another device: no remote copies, remote signals or barrier semaphores. Data moves between devices by JAX's collectives and lax.ppermute only.
A program may use at most 128 MiB of HBM per device.

```python
import jax
import jax.numpy as jnp
from jax import lax

D = 2048
H = 384
SH = 384
EXPERTS = 64
TOP = 8
GROUPS = 8
GROUP_LIMIT = 4
TOK_DEV = 64
TOKENS = 16384
CAP = 11
N_DP = 4


def draw_expert_ids(key, part):
    key = jax.random.fold_in(key, 7)
    per_group = EXPERTS // GROUPS
    hot_count = CAP * per_group // 2
    sources = TOKENS // TOK_DEV
    hot_group = jax.random.randint(jax.random.fold_in(key, 1), (), 0, GROUPS, dtype=jnp.int32)

    def one_source(subkey):
        key_order, key_perm, key_shuffle = jax.random.split(subkey, 3)
        other_groups = (hot_group + 1 + jax.random.permutation(key_order, GROUPS - 1)) % GROUPS
        positions = jnp.arange(TOK_DEV, dtype=jnp.int32)
        takes_hot = positions < hot_count
        count_rest = jnp.where(takes_hot, GROUP_LIMIT - 1, GROUP_LIMIT)
        cycle_start = jnp.cumsum(count_rest) - count_rest
        cycle_pos = (cycle_start[:, None] + jnp.arange(GROUP_LIMIT, dtype=jnp.int32)[None, :]) % (GROUPS - 1)
        picked = other_groups[cycle_pos]
        hot_column = jnp.full((TOK_DEV, 1), hot_group, jnp.int32)
        with_hot = jnp.concatenate([hot_column, picked[:, :GROUP_LIMIT - 1]], 1)
        groups_used = jnp.where(takes_hot[:, None], with_hot, picked).astype(jnp.int32)
        member = jnp.sum((groups_used[:, :, None] == jnp.arange(GROUPS, dtype=jnp.int32)[None, None, :]).astype(jnp.int32), 1)
        before = jnp.cumsum(member, 0) - member
        group_rank = jnp.take_along_axis(before, groups_used, 1)
        group_perms = jax.vmap(lambda each_key: jax.random.permutation(each_key, per_group))(jax.random.split(key_perm, GROUPS))
        first_pick = group_perms[groups_used, 2 * group_rank % per_group]
        second_pick = group_perms[groups_used, (2 * group_rank + 1) % per_group]
        expert_list = groups_used[:, :, None] * per_group + jnp.stack([first_pick, second_pick], 2)
        expert_list = expert_list.reshape(TOK_DEV, TOP)
        return expert_list[jax.random.permutation(key_shuffle, TOK_DEV)]
    return jax.vmap(one_source)(jax.random.split(key, sources)).reshape(TOKENS, TOP).astype(jnp.int32)


def plant(drawn, own_key, smallest, top_value):
    extent = drawn.shape
    place = [jax.random.randint(jax.random.fold_in(own_key, axis), (), 0, extent[axis]) for axis in range(len(extent))]
    drawn = drawn.at[tuple(place)].set(smallest)
    longest = extent.index(max(extent))
    place[longest] = (place[longest] + 1) % extent[longest]
    return drawn.at[tuple(place)].set(top_value)


def level_of(rng, extent, cuts, smallest, top_value):
    level, own = 1.0, jax.random.fold_in(rng, 6)
    for dim, shards_of in cuts:
        steps = jnp.exp(jax.random.uniform(jax.random.fold_in(own, dim), (shards_of,), jnp.float32, smallest / len(cuts), top_value / len(cuts)))
        level = level * jnp.repeat(steps, extent[dim] // shards_of).reshape([-1 if axis == dim else 1 for axis in range(len(extent))])
    return level


def noise(stream_key, shape, width, bound, cuts=(), held_as=jnp.bfloat16):
    result = jax.random.normal(stream_key, shape, jnp.float32) * width
    if len(cuts) > 0:
        result = level_of(stream_key, shape, cuts, -0.22, 0.18) * result
    return jnp.clip(result, min=-bound, max=bound).astype(held_as)


def setup_inputs(seed: int = 0) -> dict:
    key_list = jax.random.split(jax.random.key(seed), 11)
    return {
        "tokens": noise(key_list[0], (TOKENS, D), 1.0, 6.0, ((0, 256),)),
        "expert_ids": draw_expert_ids(jax.random.fold_in(key_list[10], 71), 0),
        "gate_numer": plant(jax.random.randint(key_list[2], (TOKENS, TOP), 1, 65), jax.random.fold_in(key_list[2], 1), 1, 64).astype(jnp.int32),
        "w_gate": noise(key_list[3], (EXPERTS, D, H), D ** -0.5, 0.125, ((0, 64),)),
        "w_up": noise(key_list[4], (EXPERTS, D, H), D ** -0.5, 0.125, ((0, 64),)),
        "w_down": noise(key_list[5], (EXPERTS, H, D), H ** -0.5, 0.3125, ((0, 64),)),
        "shared_gate": noise(key_list[6], (D, SH), D ** -0.5, 0.125),
        "shared_up": noise(key_list[7], (D, SH), D ** -0.5, 0.125),
        "shared_down": noise(key_list[8], (SH, D), SH ** -0.5, 0.3125),
        "d_out": noise(key_list[9], (TOKENS, D), 1.0, 6.0, ((0, 256),)),
    }


gate_scale = 1.0 / 64.0


def contract_last(left, right):
    return lax.dot_general(left, right, (((1,), (1,)), ((), ())), preferred_element_type=jnp.float32)


def silu_pieces(pre_gate):
    sigmoid_val = jax.nn.sigmoid(pre_gate)
    activation = pre_gate * sigmoid_val
    return activation, sigmoid_val + activation * (1.0 - sigmoid_val)


def replica_sum(left, right):
    left_parts = left.reshape(N_DP, -1, left.shape[1]).astype(jnp.float32)
    right_parts = right.reshape(N_DP, -1, right.shape[1]).astype(jnp.float32)
    partial_sums = jnp.einsum("rnd,rnh->rdh", left_parts, right_parts)
    rounded = lax.optimization_barrier(partial_sums.astype(jnp.bfloat16))
    return jnp.sum(rounded.astype(jnp.float32), 0)


def reference(tokens, expert_ids, gate_numer, w_gate, w_up, w_down, shared_gate, shared_up, shared_down, d_out):
    sources = TOKENS // TOK_DEV
    pair_count = TOK_DEV * TOP
    flat_ids = expert_ids.reshape(sources, pair_count)
    onehot = (flat_ids[:, :, None] == jnp.arange(EXPERTS, dtype=jnp.int32)[None, None, :]).astype(jnp.int32)
    slot_rank = jnp.sum((jnp.cumsum(onehot, 1) - onehot) * onehot, 2)
    source_index = jnp.arange(sources, dtype=jnp.int32)[:, None]
    token_index = (source_index * TOK_DEV + jnp.arange(pair_count, dtype=jnp.int32)[None, :] // TOP).astype(jnp.int32)
    row_index = (source_index * CAP + slot_rank).astype(jnp.int32)
    table = jnp.full((EXPERTS, sources * CAP), TOKENS, jnp.int32).at[flat_ids, row_index].set(token_index)
    gate_values = gate_numer.reshape(sources, pair_count).astype(jnp.float32) * gate_scale
    gate_table = jnp.zeros((EXPERTS, sources * CAP), jnp.float32).at[flat_ids, row_index].set(gate_values)
    padding = jnp.zeros((1, D), jnp.bfloat16)
    tokens_pad = jnp.concatenate([tokens, padding], 0)
    cotangent_pad = jnp.concatenate([d_out, padding], 0)

    def per_expert(carry, inputs):
        mixed_acc, input_acc = carry
        slot_tokens, slot_gates, gate_mat, up_mat, down_mat = inputs
        slot_rows = tokens_pad[slot_tokens]
        pre_gate = jnp.dot(slot_rows, gate_mat, preferred_element_type=jnp.float32)
        pre_up = jnp.dot(slot_rows, up_mat, preferred_element_type=jnp.float32)
        activation, act_slope = silu_pieces(pre_gate)
        hidden = (activation * pre_up).astype(jnp.bfloat16)
        expert_out = jnp.dot(hidden, down_mat, preferred_element_type=jnp.float32).astype(jnp.bfloat16)
        mixed_acc = mixed_acc.at[slot_tokens].add(slot_gates[:, None] * expert_out.astype(jnp.float32))
        slot_grads = (slot_gates[:, None] * cotangent_pad[slot_tokens].astype(jnp.float32)).astype(jnp.bfloat16)
        d_hidden = contract_last(slot_grads, down_mat)
        d_gate = (d_hidden * pre_up * act_slope).astype(jnp.bfloat16)
        d_up = (d_hidden * activation).astype(jnp.bfloat16)
        d_rows = (contract_last(d_gate, gate_mat) + contract_last(d_up, up_mat)).astype(jnp.bfloat16)
        input_acc = input_acc.at[slot_tokens].add(d_rows.astype(jnp.float32))
        grads = (replica_sum(slot_rows, d_gate), replica_sum(slot_rows, d_up), replica_sum(hidden, slot_grads))
        return (mixed_acc, input_acc), grads

    start = (jnp.zeros((TOKENS + 1, D), jnp.float32), jnp.zeros((TOKENS + 1, D), jnp.float32))
    (mixed_acc, input_acc), (grad_gate, grad_up, grad_down) = lax.scan(
        per_expert, start, (table, gate_table, w_gate, w_up, w_down))
    shared_pre_gate = jnp.dot(tokens, shared_gate, preferred_element_type=jnp.float32)
    shared_pre_up = jnp.dot(tokens, shared_up, preferred_element_type=jnp.float32)
    shared_act, shared_slope = silu_pieces(shared_pre_gate)
    shared_hidden = (shared_act * shared_pre_up).astype(jnp.bfloat16)
    shared_out = jnp.dot(shared_hidden, shared_down, preferred_element_type=jnp.float32)
    mixed = (shared_out + mixed_acc[:TOKENS]).astype(jnp.bfloat16)
    shared_d_hidden = contract_last(d_out, shared_down)
    shared_d_gate = (shared_d_hidden * shared_pre_up * shared_slope).astype(jnp.bfloat16)
    shared_d_up = (shared_d_hidden * shared_act).astype(jnp.bfloat16)
    d_tokens = (contract_last(shared_d_gate, shared_gate) + contract_last(shared_d_up, shared_up)
                + input_acc[:TOKENS]).astype(jnp.bfloat16)
    return mixed, d_tokens, grad_gate, grad_up, grad_down
```

```python
import jax
import jax.numpy as jnp
from jax import lax
from jax.sharding import Mesh, PartitionSpec as P

CAP = 11
GATE_SCALE = 1.0 / 64.0
F32 = jnp.float32
BF16 = jnp.bfloat16
OFFSETS = (0, -1, 1, -2, 2, -3, 3, 4)


def dot(left, right):
    return jnp.dot(left, right, preferred_element_type=F32)


def contract_last(left, right):
    return lax.dot_general(left, right, (((1,), (1,)), ((), ())), preferred_element_type=F32)


def contract_first(left, right):
    return lax.dot_general(left, right, (((0,), (0,)), ((), ())), preferred_element_type=F32)


def silu_pieces(pre_gate):
    sigmoid_val = jax.nn.sigmoid(pre_gate)
    activation = pre_gate * sigmoid_val
    return (activation, sigmoid_val + activation * (1.0 - sigmoid_val))


def shift(value, axis, step):
    size = lax.axis_size(axis)
    return lax.ppermute(value, axis, [(s, (s + step) % size) for s in range(size)])


def ring_gather(rows, half):
    up = down = rows
    pieces = [rows]
    for _ in range(3):
        up, down = shift(up, "z", 1), shift(down, "z", -1)
        pieces += [up, down]
    pieces.append(jnp.concatenate([shift(up[:half], "z", 1), shift(down[half:], "z", -1)]))
    return pieces


def add_round(left, right):
    return (left.astype(F32) + right.astype(F32)).astype(BF16)


def ring_scatter(blocks):
    own, m1, p1, m2, p2, m3, p3, far = blocks
    half = far.shape[0] // 2
    up4, down4 = shift(far[:half], "z", 1), shift(far[half:], "z", -1)
    up = jnp.concatenate([add_round(p3[:half], up4), p3[half:]])
    down = jnp.concatenate([m3[:half], add_round(m3[half:], down4)])
    for plus, minus in ((p2, m2), (p1, m1)):
        up = add_round(shift(up, "z", 1), plus)
        down = add_round(shift(down, "z", -1), minus)
    return shift(up, "z", 1).astype(F32) + shift(down, "z", -1).astype(F32) + own.astype(F32)


def routing(meta, tok_count):
    sources = meta.shape[0]
    z = lax.axis_index("z")
    targets = lax.axis_size("x") * lax.axis_size("core")
    k = jnp.arange(targets)
    expert = ((k // 2) * 16 + 2 * z + k % 2).astype(F32)
    ids = meta[:, :, :tok_count].astype(F32)
    gates = meta[:, :, tok_count:].astype(F32) * GATE_SCALE
    match = ids[None] == expert[:, None, None, None]
    member = jnp.any(match, 2).astype(BF16)
    gate = jnp.sum(jnp.where(match, gates[None], 0.0), 2).astype(BF16)
    before = (jnp.arange(tok_count)[:, None] < jnp.arange(tok_count)[None, :]).astype(BF16)
    rank = jnp.einsum("kst,tu->ksu", member, before, preferred_element_type=F32)
    code = jnp.where(member > 0, rank + CAP * jnp.arange(sources, dtype=F32)[None, :, None], -1.0)
    code = code.reshape(targets, 1, sources * tok_count)
    slot = jnp.arange(sources * CAP, dtype=F32)[None, :, None]
    hit = code == slot
    place = hit.astype(BF16).reshape(targets * sources * CAP, sources * tok_count)
    gated = jnp.where(hit, gate.reshape(targets, 1, sources * tok_count), 0).astype(BF16)
    return place, gated.reshape(place.shape)


def exchange(rows):
    shape = rows.shape
    return lax.all_to_all(rows.reshape(8, shape[0] // 8, shape[1]), ("x", "core"), 0, 0, tiled=True).reshape(shape)


def scatter_dp(value):
    me = lax.axis_index("dp")
    block = lambda k: lax.dynamic_index_in_dim(value, (me + k) % 4, 0, keepdims=False)
    far, plus, minus, own = block(2), block(1), block(3), block(0)
    half = far.shape[0] // 2
    up2, down2 = shift(far[:half], "dp", 1), shift(far[half:], "dp", -1)
    up = jnp.concatenate([add_round(plus[:half], up2), plus[half:]])
    down = jnp.concatenate([minus[:half], add_round(minus[half:], down2)])
    return shift(up, "dp", 1).astype(F32) + shift(down, "dp", -1).astype(F32) + own.astype(F32)


def body(tokens, expert_ids, gate_numer, w_gate, w_up, w_down, shared_gate, shared_up, shared_down, d_out):
    tok_count, width = tokens.shape
    w_gate, w_up, w_down = w_gate[0], w_up[0], w_down[0]
    meta = jnp.concatenate([expert_ids.T, gate_numer.T], 1).astype(BF16)
    meta = jnp.pad(meta, ((0, 0), (0, width - meta.shape[1])))
    payload = jnp.concatenate([tokens, meta])
    pieces = ring_gather(payload, 32)
    grads_in = ring_gather(d_out, 32)

    place, gated = routing(jnp.stack([p[tok_count:, : 2 * tok_count] for p in pieces]), tok_count)
    rows = exchange(dot(place, jnp.concatenate([p[:tok_count] for p in pieces])).astype(BF16))
    slot_grads = exchange(dot(gated, jnp.concatenate(grads_in)).astype(BF16))

    pre_gate, pre_up = dot(rows, w_gate), dot(rows, w_up)
    activation, slope = silu_pieces(pre_gate)
    hidden = (activation * pre_up).astype(BF16)
    out_rows = exchange(dot(hidden, w_down).astype(BF16))

    d_hidden = contract_last(slot_grads, w_down)
    d_gate = (d_hidden * pre_up * slope).astype(BF16)
    d_up = (d_hidden * activation).astype(BF16)
    d_rows = exchange((contract_last(d_gate, w_gate) + contract_last(d_up, w_up)).astype(BF16))

    mixed = ring_scatter(jnp.split(contract_first(gated, out_rows).astype(BF16), 8))
    d_in = ring_scatter(jnp.split(contract_first(place, d_rows).astype(BF16), 8))

    grad_gate = scatter_dp(contract_first(rows, d_gate).astype(BF16).reshape(4, width // 4, -1))
    grad_up = scatter_dp(contract_first(rows, d_up).astype(BF16).reshape(4, width // 4, -1))
    grad_down = contract_first(slot_grads, hidden).astype(BF16)
    grad_down = scatter_dp(grad_down.reshape(4, width // 4, -1)).T

    shared_pre_gate, shared_pre_up = dot(tokens, shared_gate), dot(tokens, shared_up)
    shared_act, shared_slope = silu_pieces(shared_pre_gate)
    shared_hidden = (shared_act * shared_pre_up).astype(BF16)
    shared_out = dot(shared_hidden, shared_down)
    shared_d_hidden = contract_last(d_out, shared_down)
    shared_d_gate = (shared_d_hidden * shared_pre_up * shared_slope).astype(BF16)
    shared_d_up = (shared_d_hidden * shared_act).astype(BF16)
    shared_d_in = contract_last(shared_d_gate, shared_gate) + contract_last(shared_d_up, shared_up)
    return (
        (shared_out + mixed).astype(BF16),
        (shared_d_in + d_in).astype(BF16),
        grad_gate[None],
        grad_up[None],
        grad_down[None],
    )


def solution(mesh):
    fine = Mesh(mesh.devices.reshape(4, 4, 8, 2), ("dp", "x", "z", "core"))
    every = P(("dp", "x", "z", "core"), None)
    expert = P(("x", "z", "core"), None, None)
    return jax.shard_map(
        body,
        mesh=fine,
        in_specs=(every, every, every, expert, expert, expert, P(), P(), P(), every),
        out_specs=(
            every,
            every,
            P(("x", "z", "core"), "dp", None),
            P(("x", "z", "core"), "dp", None),
            P(("x", "z", "core"), None, "dp"),
        ),
        check_vma=False,
    )
```

```python
import jax
import jax.numpy as jnp
from jax import lax
from jax.experimental import pallas as pl
from jax.experimental.pallas import tpu as pltpu
from jax.sharding import Mesh, PartitionSpec as P

CAP = 11
GATE_SCALE = 1.0 / 64.0
F32 = jnp.float32
BF16 = jnp.bfloat16
def dot(left, right):
    return jnp.dot(left, right, preferred_element_type=F32)


def contract_last(left, right):
    return lax.dot_general(left, right, (((1,), (1,)), ((), ())), preferred_element_type=F32)


def contract_first(left, right):
    return lax.dot_general(left, right, (((0,), (0,)), ((), ())), preferred_element_type=F32)


def silu_pieces(pre_gate):
    sigmoid_val = jax.nn.sigmoid(pre_gate)
    activation = pre_gate * sigmoid_val
    return (activation, sigmoid_val + activation * (1.0 - sigmoid_val))


def ring_step(value, step):
    size = lax.axis_size("z")
    pairs = [(2 * s + c, 2 * ((s + step * (1 - 2 * c)) % size) + c) for s in range(size) for c in range(2)]
    return lax.ppermute(value, ("z", "core"), pairs)


def dp_step(value, step):
    size = lax.axis_size("dp")
    pairs = [(2 * s + c, 2 * ((s + step * (1 - 2 * c)) % size) + c) for s in range(size) for c in range(2)]
    return lax.ppermute(value, ("dp", "core"), pairs)


def ring_gather(rows):
    ahead = behind = rows
    pieces = [rows]
    for _ in range(3):
        ahead, behind = ring_step(ahead, 1), ring_step(behind, -1)
        pieces += [ahead, behind]
    return pieces + [ring_step(ahead, 1)]


def add(left, right):
    return (left.astype(F32) + right.astype(F32)).astype(BF16)


def ring_scatter(blocks):
    own, a1, b1, a2, b2, a3, b3, a4 = blocks
    ahead, behind = add(ring_step(a4, -1), a3), b3
    for a, b in ((a2, b2), (a1, b1)):
        ahead, behind = add(ring_step(ahead, -1), a), add(ring_step(behind, 1), b)
    return (ring_step(ahead, -1), ring_step(behind, 1), own), (ahead, behind)


def total(terms):
    return sum(t.astype(F32) for t in terms)


SOURCES = 8
TARGETS = 8
SLOTS = SOURCES * CAP
META = 128


def select_kernel(z, *refs):
    pieces, metas = refs[:SOURCES], refs[SOURCES : 2 * SOURCES]
    rows, place, gated = refs[2 * SOURCES :]
    toks = pieces[0].shape[0]
    cols = SOURCES * toks

    @pl.when(pl.program_id(0) == 0)
    def _():
        meta = jnp.concatenate([m[...] for m in metas], 0).astype(F32).T
        ids, gates = meta[:8], meta[8:16] * GATE_SCALE
        lane = lax.broadcasted_iota(jnp.int32, (cols, cols), 1)
        sub = lax.broadcasted_iota(jnp.int32, (cols, cols), 0)
        before = jnp.where((sub < lane) & (sub >= (lane // toks) * toks), 1.0, 0.0).astype(BF16)
        member, gate = [], []
        for k in range(TARGETS):
            match = ids == ((k // 2) * 16 + 2 * z[0] + k % 2).astype(F32)
            member.append(jnp.max(jnp.where(match, 1.0, 0.0), 0, keepdims=True))
            gate.append(jnp.sum(jnp.where(match, gates, 0.0), 0, keepdims=True))
        member = jnp.concatenate(member, 0)
        rank = dot(member.astype(BF16), before)
        first = (lax.broadcasted_iota(jnp.int32, member.shape, 1) // toks * CAP).astype(F32)
        code = jnp.where(member > 0.0, rank + first, -1.0)
        slot = lax.broadcasted_iota(jnp.int32, (SLOTS, cols), 0).astype(F32)
        hits = [code[k : k + 1] == slot for k in range(TARGETS)]
        place[...] = jnp.concatenate([jnp.where(h, 1.0, 0.0) for h in hits], 0).astype(BF16)
        gated[...] = jnp.concatenate([jnp.where(h, g, 0.0) for h, g in zip(hits, gate)], 0).astype(BF16)

    rows[...] = dot(place[...], jnp.concatenate([p[...] for p in pieces], 0)).astype(BF16)


def pick_kernel(mat, *refs):
    refs[-1][...] = dot(mat[...], jnp.concatenate([p[...] for p in refs[:-1]], 0)).astype(BF16)


def combine_kernel(mat, rows, *outs):
    summed = dot(mat[...], rows[...]).astype(BF16)
    toks = outs[0].shape[0]
    for i, out in enumerate(outs):
        out[...] = summed[i * toks : (i + 1) * toks]


VMEM = pltpu.CompilerParams(vmem_limit_bytes=60 * 2**20)
COLUMN = 1024


def select(z, pieces, width):
    toks = pieces[0].shape[0]
    whole = pl.BlockSpec((TARGETS * SLOTS, SOURCES * toks), lambda i, z: (0, 0))
    wide = lambda rows: pl.BlockSpec((rows, COLUMN), lambda i, z: (0, i))
    return pl.pallas_call(
        select_kernel,
        grid_spec=pltpu.PrefetchScalarGridSpec(
            num_scalar_prefetch=1,
            grid=(width // COLUMN,),
            in_specs=[wide(toks)] * SOURCES + [pl.BlockSpec((toks, META), lambda i, z: (0, width // META))] * SOURCES,
            out_specs=[wide(TARGETS * SLOTS), whole, whole],
        ),
        out_shape=[jax.ShapeDtypeStruct((TARGETS * SLOTS, w), BF16) for w in (width, SOURCES * toks, SOURCES * toks)],
        compiler_params=VMEM,
        cost_estimate=pl.CostEstimate(flops=2 * TARGETS * SLOTS * SOURCES * toks * width, bytes_accessed=8 * 2**20, transcendentals=0),
    )(z, *pieces, *pieces)


def by_columns(kernel, mat, arrays, out_rows):
    width = arrays[0].shape[1]
    wide = lambda rows: pl.BlockSpec((rows, COLUMN), lambda i: (0, i))
    return pl.pallas_call(
        kernel,
        grid=(width // COLUMN,),
        in_specs=[pl.BlockSpec(mat.shape, lambda i: (0, 0))] + [wide(a.shape[0]) for a in arrays],
        out_specs=[wide(r) for r in out_rows],
        out_shape=[jax.ShapeDtypeStruct((r, width), BF16) for r in out_rows],
        compiler_params=VMEM,
        cost_estimate=pl.CostEstimate(flops=2 * mat.size * width, bytes_accessed=6 * 2**20, transcendentals=0),
    )(mat, *arrays)


def after(value, others):
    return lax.optimization_barrier((value, others))[0]


def exchange(rows, also=None):
    if also is not None:
        rows, also = lax.optimization_barrier((rows, also))
    shape = rows.shape
    got = lax.all_to_all(rows.reshape(8, shape[0] // 8, shape[1]), ("x", "core"), 0, 0, tiled=True)
    return got.reshape(shape), also


def forward_kernel(rows, w_gate, w_up, w_down, out, pre_gate, pre_up, hidden):
    gate = dot(rows[...], w_gate[...])
    up = dot(rows[...], w_up[...])
    pre_gate[...], pre_up[...] = gate, up
    hid = (silu_pieces(gate)[0] * up).astype(BF16)
    hidden[...] = hid
    out[...] = dot(hid, w_down[...]).astype(BF16)


def backward_kernel(grads, pre_gate, pre_up, w_gate, w_up, w_down, d_rows, d_gate, d_up):
    d_hidden = contract_last(grads[...], w_down[...])
    activation, slope = silu_pieces(pre_gate[...])
    gate = (d_hidden * pre_up[...] * slope).astype(BF16)
    up = (d_hidden * activation).astype(BF16)
    d_gate[...], d_up[...] = gate, up
    d_rows[...] = (contract_last(gate, w_gate[...]) + contract_last(up, w_up[...])).astype(BF16)


def strips(inner, block):
    for column in range(block // 128):
        row = 0
        while row < inner:
            at = column * inner + row
            count = min(inner - row, block - at % block)
            yield column, row, at % block, at // block, count
            row += count


def grads_kernel(order, rows, grads, hidden, d_gate, d_up, *outs):
    block, inner = rows.shape[1], hidden.shape[1]
    gate = contract_first(rows[...], d_gate[...]).astype(BF16)
    up = contract_first(rows[...], d_up[...]).astype(BF16)
    down = contract_first(hidden[...], grads[...]).astype(BF16)
    for k, out in enumerate(outs):

        @pl.when(pl.program_id(0) == k)
        def _():
            out[:block] = gate
            out[block : 2 * block] = up
            for col, row, to_row, to_col, n in strips(inner, block):
                out[2 * block + to_row : 2 * block + to_row + n, to_col * 128 : (to_col + 1) * 128] = down[
                    row : row + n, col * 128 : (col + 1) * 128
                ]


def sum_kernel(*refs):
    gate, up, down = refs[3:]
    block, inner = gate.shape[1:]
    value = total([r[...] for r in refs[:3]])
    gate[0], up[0] = value[:block], value[block : 2 * block]
    for col, row, to_row, to_col, n in strips(inner, block):
        down[0, row : row + n, col * 128 : (col + 1) * 128] = value[
            2 * block + to_row : 2 * block + to_row + n, to_col * 128 : (to_col + 1) * 128
        ]


ROW_STEPS = 2


def by_rows(kernel, count, width_in, weights, width_out):
    block = count // ROW_STEPS
    rowwise = lambda width: pl.BlockSpec((block, width), lambda i: (i, 0))
    whole = lambda shape: pl.BlockSpec(shape, lambda i: (0, 0))
    return pl.pallas_call(
        kernel,
        grid=(ROW_STEPS,),
        in_specs=[rowwise(w) for w in width_in] + [whole(s) for s in weights],
        out_specs=[rowwise(w) for w, _ in width_out],
        out_shape=[jax.ShapeDtypeStruct((count, w), t) for w, t in width_out],
        compiler_params=VMEM,
        cost_estimate=pl.CostEstimate(flops=6 * count * 2048 * 384, bytes_accessed=14 * 2**20, transcendentals=count * 384),
    )


def expert_grads(rows, grads, hidden, d_gate, d_up):
    count, width = rows.shape
    inner = hidden.shape[1]
    block = width // 4
    step = 1 - 2 * lax.axis_index("core")
    order = (lax.axis_index("dp") + step * jnp.arange(4, dtype=jnp.int32) + 4) % 4
    picked = pl.BlockSpec((count, block), lambda k, order: (0, order[k]))
    whole = pl.BlockSpec((count, inner), lambda k, order: (0, 0))
    return pl.pallas_call(
        grads_kernel,
        grid_spec=pltpu.PrefetchScalarGridSpec(
            num_scalar_prefetch=1,
            grid=(4,),
            in_specs=[picked, picked, whole, whole, whole],
            out_specs=[pl.BlockSpec((3 * block, inner), lambda k, order: (0, 0))] * 4,
        ),
        out_shape=[jax.ShapeDtypeStruct((3 * block, inner), BF16)] * 4,
        compiler_params=VMEM,
        cost_estimate=pl.CostEstimate(flops=6 * count * width * inner, bytes_accessed=12 * 2**20, transcendentals=0),
    )(order, rows, grads, hidden, d_gate, d_up)


def sum_grads(parts, block, inner):
    shapes = [(1, block, inner), (1, block, inner), (1, inner, block)]
    return pl.pallas_call(
        sum_kernel,
        out_shape=[jax.ShapeDtypeStruct(shape, F32) for shape in shapes],
        compiler_params=VMEM,
        cost_estimate=pl.CostEstimate(flops=12 * block * inner, bytes_accessed=24 * block * inner, transcendentals=0),
    )(*parts)


def body(tokens, expert_ids, gate_numer, w_gate, w_up, w_down, shared_gate, shared_up, shared_down, d_out):
    tok_count, width = tokens.shape
    w_gate, w_up, w_down = w_gate[0], w_up[0], w_down[0]
    inner = w_gate.shape[1]
    weights = (w_gate.shape, w_up.shape, w_down.shape)
    meta = jnp.concatenate([expert_ids, gate_numer], 1).astype(BF16)
    meta = jnp.pad(meta, ((0, 0), (0, META - meta.shape[1])))
    pieces = ring_gather(jnp.concatenate([tokens, meta], 1))
    grads_in = ring_gather(after(d_out, pieces[-3:-1]))

    rows, place, gated = select(lax.axis_index("z").reshape(1), pieces, width)
    rows, _ = exchange(rows)
    (slot_grads,) = by_columns(pick_kernel, gated, grads_in, (TARGETS * SLOTS,))
    slot_grads, rows = exchange(slot_grads, rows)

    count = rows.shape[0]
    out_rows, pre_gate, pre_up, hidden = by_rows(
        forward_kernel, count, (width,), weights, ((width, BF16), (inner, F32), (inner, F32), (inner, BF16))
    )(rows, w_gate, w_up, w_down)
    shared_pre_gate, shared_pre_up = dot(tokens, shared_gate), dot(tokens, shared_up)
    shared_act, shared_slope = silu_pieces(shared_pre_gate)
    shared_hidden = (shared_act * shared_pre_up).astype(BF16)
    shared_out = dot(shared_hidden, shared_down)
    shared_d_hidden = contract_last(d_out, shared_down)
    shared_d_gate = (shared_d_hidden * shared_pre_up * shared_slope).astype(BF16)
    shared_d_up = (shared_d_hidden * shared_act).astype(BF16)
    shared_d_in = contract_last(shared_d_gate, shared_gate) + contract_last(shared_d_up, shared_up)
    aside = (shared_out, shared_d_in, gated.T, place.T)
    out_rows, (slot_grads, aside) = exchange(out_rows, (slot_grads, aside))
    shared_out, shared_d_in, from_slots, from_slots_plain = aside
    d_rows, d_gate, d_up = by_rows(
        backward_kernel, count, (width, inner, inner), weights, ((width, BF16), (inner, BF16), (inner, BF16))
    )(slot_grads, pre_gate, pre_up, w_gate, w_up, w_down)
    grads = expert_grads(rows, slot_grads, hidden, d_gate, d_up)
    d_rows, (out_rows, grads) = exchange(d_rows, (out_rows, grads))

    split = (tok_count,) * SOURCES
    mixed, _ = ring_scatter(by_columns(combine_kernel, from_slots, (out_rows,), split))
    far, near = dp_step(grads[2], 1), dp_step(grads[3], -1)
    d_rows = after(d_rows, (mixed, far, near))
    far = dp_step(add(far, grads[1]), 1)
    d_in, early = ring_scatter(by_columns(combine_kernel, from_slots_plain, (d_rows,), split))
    parts = after([grads[0], far, near], early)
    grad_gate, grad_up, grad_down = sum_grads(parts, width // 4, inner)

    return (
        (shared_out + total(mixed)).astype(BF16),
        (shared_d_in + total(d_in)).astype(BF16),
        grad_gate,
        grad_up,
        grad_down,
    )


def solution(mesh):
    fine = Mesh(mesh.devices.reshape(4, 4, 8, 2), ("dp", "x", "z", "core"))
    every = P(("dp", "x", "z", "core"), None)
    expert = P(("x", "z", "core"), None, None)
    return jax.shard_map(
        body,
        mesh=fine,
        in_specs=(every, every, every, expert, expert, expert, P(), P(), P(), every),
        out_specs=(
            every,
            every,
            P(("x", "z", "core"), "dp", None),
            P(("x", "z", "core"), "dp", None),
            P(("x", "z", "core"), None, "dp"),
        ),
        check_vma=False,
    )
```

```python
import jax
import jax.numpy as jnp
from jax import lax
from jax.experimental import pallas as pl
from jax.experimental.pallas import tpu as pltpu
from jax.sharding import Mesh, PartitionSpec as P

CAP = 11
GATE_SCALE = 1.0 / 64.0
F32 = jnp.float32
BF16 = jnp.bfloat16
def dot(left, right):
    return jnp.dot(left, right, preferred_element_type=F32)


def contract_last(left, right):
    return lax.dot_general(left, right, (((1,), (1,)), ((), ())), preferred_element_type=F32)


def contract_first(left, right):
    return lax.dot_general(left, right, (((0,), (0,)), ((), ())), preferred_element_type=F32)


def silu_pieces(pre_gate):
    sigmoid_val = jax.nn.sigmoid(pre_gate)
    activation = pre_gate * sigmoid_val
    return (activation, sigmoid_val + activation * (1.0 - sigmoid_val))


def ring_step(value, step):
    size = lax.axis_size("z")
    pairs = [(2 * s + c, 2 * ((s + step * (1 - 2 * c)) % size) + c) for s in range(size) for c in range(2)]
    return lax.ppermute(value, ("z", "core"), pairs)


def dp_step(value, step):
    size = lax.axis_size("dp")
    return lax.ppermute(value, "dp", [(s, (s + step) % size) for s in range(size)])


def ring_gather(parts):
    ahead = behind = parts
    pieces = [parts]
    for _ in range(3):
        hops = [(ring_step(p, 1), ring_step(q, -1)) for p, q in zip(ahead, behind)]
        ahead, behind = zip(*hops)
        pieces += [ahead, behind]
    return pieces + [tuple(ring_step(p, 1) for p in ahead)]


def add(left, right):
    return (left.astype(F32) + right.astype(F32)).astype(BF16)


def ring_scatter(blocks):
    own, a1, b1, a2, b2, a3, b3, a4 = blocks
    ahead, behind = add(ring_step(a4, -1), a3), b3
    for a, b in ((a2, b2), (a1, b1)):
        ahead, behind = add(ring_step(ahead, -1), a), add(ring_step(behind, 1), b)
    return (ring_step(ahead, -1), ring_step(behind, 1), own), (ahead, behind)


def total(terms):
    return sum(t.astype(F32) for t in terms)


SOURCES = 8
TARGETS = 8
SLOTS = SOURCES * CAP
META = 128


def select_kernel(z, *refs):
    count = (len(refs) - 3) // 2
    pieces, metas = refs[:count], refs[count : 2 * count]
    rows, place, gated = refs[2 * count :]
    cols = place.shape[1]
    toks = cols // SOURCES

    @pl.when(pl.program_id(0) == 0)
    def _():
        meta = jnp.concatenate([m[...] for m in metas], 0).astype(F32).T
        ids, gates = meta[:8], meta[8:16] * GATE_SCALE
        lane = lax.broadcasted_iota(jnp.int32, (cols, cols), 1)
        sub = lax.broadcasted_iota(jnp.int32, (cols, cols), 0)
        before = jnp.where((sub < lane) & (sub >= (lane // toks) * toks), 1.0, 0.0).astype(BF16)
        member, gate = [], []
        for k in range(TARGETS):
            match = ids == ((k // 2) * 16 + 2 * z[0] + k % 2).astype(F32)
            member.append(jnp.max(jnp.where(match, 1.0, 0.0), 0, keepdims=True))
            gate.append(jnp.sum(jnp.where(match, gates, 0.0), 0, keepdims=True))
        member = jnp.concatenate(member, 0)
        rank = dot(member.astype(BF16), before)
        first = (lax.broadcasted_iota(jnp.int32, member.shape, 1) // toks * CAP).astype(F32)
        code = jnp.where(member > 0.0, rank + first, -1.0)
        slot = lax.broadcasted_iota(jnp.int32, (SLOTS, cols), 0).astype(F32)
        hits = [code[k : k + 1] == slot for k in range(TARGETS)]
        place[...] = jnp.concatenate([jnp.where(h, 1.0, 0.0) for h in hits], 0).astype(BF16)
        gated[...] = jnp.concatenate([jnp.where(h, g, 0.0) for h, g in zip(hits, gate)], 0).astype(BF16)

    rows[...] = dot(place[...], jnp.concatenate([p[...] for p in pieces], 0)).astype(BF16)


def pick_kernel(mat, *refs):
    refs[-1][...] = dot(mat[...], jnp.concatenate([p[...] for p in refs[:-1]], 0)).astype(BF16)


def combine_kernel(mat, rows, *outs):
    summed = dot(mat[...], rows[...]).astype(BF16)
    toks = outs[0].shape[0]
    for i, out in enumerate(outs):
        out[...] = summed[i * toks : (i + 1) * toks]


VMEM = pltpu.CompilerParams(vmem_limit_bytes=60 * 2**20)
COLUMN = 1024


def select(z, pieces, width):
    part, count = pieces[0].shape[0], len(pieces)
    cols = part * count
    whole = pl.BlockSpec((TARGETS * SLOTS, cols), lambda i, z: (0, 0))
    wide = lambda rows: pl.BlockSpec((rows, COLUMN), lambda i, z: (0, i))
    return pl.pallas_call(
        select_kernel,
        grid_spec=pltpu.PrefetchScalarGridSpec(
            num_scalar_prefetch=1,
            grid=(width // COLUMN,),
            in_specs=[wide(part)] * count + [pl.BlockSpec((part, META), lambda i, z: (0, width // META))] * count,
            out_specs=[wide(TARGETS * SLOTS), whole, whole],
        ),
        out_shape=[jax.ShapeDtypeStruct((TARGETS * SLOTS, w), BF16) for w in (width, cols, cols)],
        compiler_params=VMEM,
        cost_estimate=pl.CostEstimate(flops=2 * TARGETS * SLOTS * cols * width, bytes_accessed=8 * 2**20, transcendentals=0),
    )(z, *pieces, *pieces)


def by_columns(kernel, mat, arrays, out_rows):
    width = arrays[0].shape[1]
    wide = lambda rows: pl.BlockSpec((rows, COLUMN), lambda i: (0, i))
    return pl.pallas_call(
        kernel,
        grid=(width // COLUMN,),
        in_specs=[pl.BlockSpec(mat.shape, lambda i: (0, 0))] + [wide(a.shape[0]) for a in arrays],
        out_specs=[wide(r) for r in out_rows],
        out_shape=[jax.ShapeDtypeStruct((r, width), BF16) for r in out_rows],
        compiler_params=VMEM,
        cost_estimate=pl.CostEstimate(flops=2 * mat.size * width, bytes_accessed=6 * 2**20, transcendentals=0),
    )(mat, *arrays)


def after(value, others):
    return lax.optimization_barrier((value, others))[0]


def exchange(rows, also=None):
    if also is not None:
        rows, also = lax.optimization_barrier((rows, also))
    shape = rows.shape
    got = lax.all_to_all(rows.reshape(8, shape[0] // 8, shape[1]), ("x", "core"), 0, 0, tiled=True)
    return got.reshape(shape), also


def forward_kernel(rows, w_in, w_down, out, pre, hidden):
    inner = hidden.shape[1]
    both = dot(rows[...], w_in[...])
    pre[...] = both
    hid = (silu_pieces(both[:, :inner])[0] * both[:, inner:]).astype(BF16)
    hidden[...] = hid
    out[...] = dot(hid, w_down[...]).astype(BF16)


def backward_kernel(grads, pre, w_in, w_down, d_rows, d_pre):
    inner = w_down.shape[0]
    d_hidden = contract_last(grads[...], w_down[...])
    activation, slope = silu_pieces(pre[:, :inner])
    gate = (d_hidden * pre[:, inner:] * slope).astype(BF16)
    up = (d_hidden * activation).astype(BF16)
    both = jnp.concatenate([gate, up], 1)
    d_pre[...] = both
    d_rows[...] = contract_last(both, w_in[...]).astype(BF16)


def strips(inner, block):
    for column in range(block // 128):
        row = 0
        while row < inner:
            at = column * inner + row
            count = min(inner - row, block - at % block)
            yield column, row, at % block, at // block, count
            row += count


def grads_kernel(order, rows, grads, hidden, d_pre, *refs):
    outs, turned = refs[:-1], refs[-1]
    block, inner = rows.shape[1], hidden.shape[1]

    @pl.when(pl.program_id(0) == 0)
    def _():
        turned[...] = hidden[...].astype(F32).T.astype(BF16)

    both = contract_first(rows[...], d_pre[...]).astype(BF16)
    down = dot(turned[...], grads[...]).astype(BF16)
    for k, out in enumerate(outs):

        @pl.when(pl.program_id(0) == k)
        def _():
            out[:block] = both[:, :inner]
            out[block : 2 * block] = both[:, inner:]
            for col, row, to_row, to_col, n in strips(inner, block):
                out[2 * block + to_row : 2 * block + to_row + n, to_col * 128 : (to_col + 1) * 128] = down[
                    row : row + n, col * 128 : (col + 1) * 128
                ]


def sum_kernel(*refs):
    gate, up, down = refs[3:]
    block, inner = gate.shape[1:]
    value = total([r[...] for r in refs[:3]])
    gate[0], up[0] = value[:block], value[block : 2 * block]
    for col, row, to_row, to_col, n in strips(inner, block):
        down[0, row : row + n, col * 128 : (col + 1) * 128] = value[
            2 * block + to_row : 2 * block + to_row + n, to_col * 128 : (to_col + 1) * 128
        ]


ROW_STEPS = 2


def by_rows(kernel, arrays, weights, outs):
    rowwise = lambda rows, width: pl.BlockSpec((rows // ROW_STEPS, width), lambda i: (i, 0))
    whole = lambda shape: pl.BlockSpec(shape, lambda i: (0, 0))
    count = arrays[0].shape[0]
    return pl.pallas_call(
        kernel,
        grid=(ROW_STEPS,),
        in_specs=[rowwise(*a.shape) for a in arrays] + [whole(w.shape) for w in weights],
        out_specs=[rowwise(r, w) for r, w, _ in outs],
        out_shape=[jax.ShapeDtypeStruct((r, w), t) for r, w, t in outs],
        compiler_params=VMEM,
        cost_estimate=pl.CostEstimate(flops=6 * count * 2048 * 384, bytes_accessed=14 * 2**20, transcendentals=count * 384),
    )(*arrays, *weights)


def expert_grads(rows, grads, hidden, d_pre, hops):
    count, width = rows.shape
    inner = hidden.shape[1]
    block = width // 4
    order = (lax.axis_index("dp") + jnp.array(hops, jnp.int32)) % 4
    picked = pl.BlockSpec((count, block), lambda k, order: (0, order[k]))
    whole = lambda a: pl.BlockSpec(a.shape, lambda k, order: (0, 0))
    return pl.pallas_call(
        grads_kernel,
        grid_spec=pltpu.PrefetchScalarGridSpec(
            num_scalar_prefetch=1,
            grid=(len(hops),),
            in_specs=[picked, picked, whole(hidden), whole(d_pre)],
            out_specs=[pl.BlockSpec((3 * block, inner), lambda k, order: (0, 0))] * len(hops),
            scratch_shapes=[pltpu.VMEM((inner, count), BF16)],
        ),
        out_shape=[jax.ShapeDtypeStruct((3 * block, inner), BF16)] * len(hops),
        compiler_params=VMEM,
        cost_estimate=pl.CostEstimate(flops=6 * count * block * inner * len(hops), bytes_accessed=6 * 2**20, transcendentals=0),
    )(order, rows, grads, hidden, d_pre)


def sum_grads(parts, block, inner):
    shapes = [(1, block, inner), (1, block, inner), (1, inner, block)]
    return pl.pallas_call(
        sum_kernel,
        out_shape=[jax.ShapeDtypeStruct(shape, F32) for shape in shapes],
        compiler_params=VMEM,
        cost_estimate=pl.CostEstimate(flops=12 * block * inner, bytes_accessed=24 * block * inner, transcendentals=0),
    )(*parts)


def body(tokens, expert_ids, gate_numer, w_gate, w_up, w_down, shared_gate, shared_up, shared_down, d_out):
    tok_count, width = tokens.shape
    w_gate, w_up, w_down = w_gate[0], w_up[0], w_down[0]
    inner = w_gate.shape[1]
    w_in = jnp.concatenate([w_gate, w_up], 1)
    meta = jnp.concatenate([expert_ids, gate_numer], 1).astype(BF16)
    meta = jnp.pad(meta, ((0, 0), (0, META - meta.shape[1])))
    payload = jnp.concatenate([tokens, meta], 1)
    pieces = ring_gather((payload[: tok_count // 2], payload[tok_count // 2 :]))
    grads_in = [p for (p,) in ring_gather((after(d_out, pieces[-3:-1]),))]
    pieces = [p for halves in pieces for p in halves]

    rows, place, gated = select(lax.axis_index("z").reshape(1), pieces, width)
    rows, _ = exchange(after(rows, grads_in[1:3]))
    (slot_grads,) = by_columns(pick_kernel, gated, grads_in, (TARGETS * SLOTS,))
    slot_grads, rows = exchange(slot_grads, rows)

    count = rows.shape[0]
    out_rows, pre, hidden = by_rows(
        forward_kernel,
        (rows,),
        (w_in, w_down),
        ((count, width, BF16), (count, 2 * inner, F32), (count, inner, BF16)),
    )
    shared_pre_gate, shared_pre_up = dot(tokens, shared_gate), dot(tokens, shared_up)
    shared_act, shared_slope = silu_pieces(shared_pre_gate)
    shared_hidden = (shared_act * shared_pre_up).astype(BF16)
    shared_out = dot(shared_hidden, shared_down)
    shared_d_hidden = contract_last(d_out, shared_down)
    shared_d_gate = (shared_d_hidden * shared_pre_up * shared_slope).astype(BF16)
    shared_d_up = (shared_d_hidden * shared_act).astype(BF16)
    shared_d_in = contract_last(shared_d_gate, shared_gate) + contract_last(shared_d_up, shared_up)
    aside = (shared_out, shared_d_in, gated.T, place.T)
    out_rows, (slot_grads, aside) = exchange(out_rows, (slot_grads, aside))
    shared_out, shared_d_in, out_mat, in_mat = aside
    d_rows, d_pre = by_rows(
        backward_kernel,
        (slot_grads, pre),
        (w_in, w_down),
        ((count, width, BF16), (count, 2 * inner, BF16)),
    )
    (two_on,) = expert_grads(rows, slot_grads, hidden, d_pre, (2,))
    half = two_on.shape[0] // 2
    ahead_2, behind_2 = dp_step(two_on[:half], 1), dp_step(two_on[half:], -1)
    ahead, behind, mine = expert_grads(rows, slot_grads, hidden, d_pre, (1, 3, 0))
    ahead = jnp.concatenate([add(ahead[:half], ahead_2), ahead[half:]])
    behind = jnp.concatenate([behind[:half], add(behind[half:], behind_2)])
    d_rows, (out_rows, ahead, behind, mine) = exchange(d_rows, (out_rows, ahead, behind, mine))

    split = (tok_count,) * SOURCES
    mixed, _ = ring_scatter(by_columns(combine_kernel, out_mat, (out_rows,), split))
    ahead, behind = dp_step(ahead, 1), dp_step(behind, -1)
    d_rows = after(d_rows, mixed)
    d_in, early = ring_scatter(by_columns(combine_kernel, in_mat, (d_rows,), split))
    parts = after([mine, ahead, behind], early)
    grad_gate, grad_up, grad_down = sum_grads(parts, width // 4, inner)

    return (
        (shared_out + total(mixed)).astype(BF16),
        (shared_d_in + total(d_in)).astype(BF16),
        grad_gate,
        grad_up,
        grad_down,
    )


def solution(mesh):
    fine = Mesh(mesh.devices.reshape(4, 4, 8, 2), ("dp", "x", "z", "core"))
    every = P(("dp", "x", "z", "core"), None)
    expert = P(("x", "z", "core"), None, None)
    return jax.shard_map(
        body,
        mesh=fine,
        in_specs=(every, every, every, expert, expert, expert, P(), P(), P(), every),
        out_specs=(
            every,
            every,
            P(("x", "z", "core"), "dp", None),
            P(("x", "z", "core"), "dp", None),
            P(("x", "z", "core"), None, "dp"),
        ),
        check_vma=False,
    )
```

```python
import jax
import jax.numpy as jnp
from jax import lax
from jax.experimental import pallas as pl
from jax.experimental.pallas import tpu as pltpu
from jax.sharding import Mesh, PartitionSpec as P

CAP = 11
GATE_SCALE = 1.0 / 64.0
F32 = jnp.float32
BF16 = jnp.bfloat16
def dot(left, right):
    return jnp.dot(left, right, preferred_element_type=F32)


def contract_last(left, right):
    return lax.dot_general(left, right, (((1,), (1,)), ((), ())), preferred_element_type=F32)


def contract_first(left, right):
    return lax.dot_general(left, right, (((0,), (0,)), ((), ())), preferred_element_type=F32)


def silu_pieces(pre_gate):
    sigmoid_val = jax.nn.sigmoid(pre_gate)
    activation = pre_gate * sigmoid_val
    return (activation, sigmoid_val + activation * (1.0 - sigmoid_val))


def ring_step(value, step):
    size = lax.axis_size("z")
    pairs = [(2 * s + c, 2 * ((s + step * (1 - 2 * c)) % size) + c) for s in range(size) for c in range(2)]
    return lax.ppermute(value, ("z", "core"), pairs)


def dp_step(value, step):
    size = lax.axis_size("dp")
    return lax.ppermute(value, "dp", [(s, (s + step) % size) for s in range(size)])


def ring_gather(parts):
    ahead = behind = parts
    pieces = [parts]
    for _ in range(3):
        hops = [(ring_step(p, 1), ring_step(q, -1)) for p, q in zip(ahead, behind)]
        ahead, behind = zip(*hops)
        pieces += [ahead, behind]
    return pieces + [tuple(ring_step(p, 1) for p in ahead)]


def add(left, right):
    return (left.astype(F32) + right.astype(F32)).astype(BF16)


def ring_scatter(far, near, before_third=()):
    b1, a2, b2, a3, b3, a4 = far
    own, a1, b1_too = near
    ahead, behind = add(ring_step(a4, -1), a3), b3
    ahead, behind = add(ring_step(ahead, -1), a2), add(ring_step(behind, 1), b2)
    ahead, behind = after((ahead, behind), before_third)
    ahead, behind = add(ring_step(ahead, -1), a1), total((ring_step(behind, 1), b1, b1_too)).astype(BF16)
    return (ring_step(ahead, -1), ring_step(behind, 1), own), (ahead, behind)


def total(terms):
    return sum(t.astype(F32) for t in terms)


SOURCES = 8
TARGETS = 8
SLOTS = SOURCES * CAP
NEAR = 32
META = 128


def select_kernel(z, *refs):
    count = (len(refs) - 3) // 2
    pieces, metas = refs[:count], refs[count : 2 * count]
    rows, place, gated = refs[2 * count :]
    cols = place.shape[1]
    toks = cols // SOURCES

    @pl.when(pl.program_id(0) == 0)
    def _():
        meta = jnp.concatenate([m[...] for m in metas], 0).astype(F32).T
        ids, gates = meta[:8], meta[8:16] * GATE_SCALE
        lane = lax.broadcasted_iota(jnp.int32, (cols, cols), 1)
        sub = lax.broadcasted_iota(jnp.int32, (cols, cols), 0)
        before = jnp.where((sub < lane) & (sub >= (lane // toks) * toks), 1.0, 0.0).astype(BF16)
        member, gate = [], []
        for k in range(TARGETS):
            match = ids == ((k // 2) * 16 + 2 * z[0] + k % 2).astype(F32)
            member.append(jnp.max(jnp.where(match, 1.0, 0.0), 0, keepdims=True))
            gate.append(jnp.sum(jnp.where(match, gates, 0.0), 0, keepdims=True))
        member = jnp.concatenate(member, 0)
        rank = dot(member.astype(BF16), before)
        first = (lax.broadcasted_iota(jnp.int32, member.shape, 1) // toks * CAP).astype(F32)
        code = jnp.where(member > 0.0, rank + first, -1.0)
        slot = lax.broadcasted_iota(jnp.int32, (SLOTS, cols), 0).astype(F32)
        hits = [code[k : k + 1] == slot for k in range(TARGETS)]
        place[...] = jnp.concatenate([jnp.where(h, 1.0, 0.0) for h in hits], 0).astype(BF16)
        gated[...] = jnp.concatenate([jnp.where(h, g, 0.0) for h, g in zip(hits, gate)], 0).astype(BF16)

    rows[...] = dot(place[...], jnp.concatenate([p[...] for p in pieces], 0)).astype(BF16)


def pick_kernel(mat, *refs):
    refs[-1][...] = dot(mat[...], jnp.concatenate([p[...] for p in refs[:-1]], 0)).astype(BF16)


def combine_kernel(mat, rows, *outs):
    summed = dot(mat[...], rows[...]).astype(BF16)
    toks = outs[0].shape[0]
    for i, out in enumerate(outs):
        out[...] = summed[i * toks : (i + 1) * toks]


VMEM = pltpu.CompilerParams(vmem_limit_bytes=60 * 2**20)
COLUMN = 1024


def select(z, pieces, width):
    part, count = pieces[0].shape[0], len(pieces)
    cols = part * count
    whole = pl.BlockSpec((TARGETS * SLOTS, cols), lambda i, z: (0, 0))
    wide = lambda rows: pl.BlockSpec((rows, COLUMN), lambda i, z: (0, i))
    return pl.pallas_call(
        select_kernel,
        grid_spec=pltpu.PrefetchScalarGridSpec(
            num_scalar_prefetch=1,
            grid=(width // COLUMN,),
            in_specs=[wide(part)] * count + [pl.BlockSpec((part, META), lambda i, z: (0, width // META))] * count,
            out_specs=[wide(TARGETS * SLOTS), whole, whole],
        ),
        out_shape=[jax.ShapeDtypeStruct((TARGETS * SLOTS, w), BF16) for w in (width, cols, cols)],
        compiler_params=VMEM,
        cost_estimate=pl.CostEstimate(flops=2 * TARGETS * SLOTS * cols * width, bytes_accessed=8 * 2**20, transcendentals=0),
    )(z, *pieces, *pieces)


def by_columns(kernel, mat, arrays, out_rows):
    width = arrays[0].shape[1]
    wide = lambda rows: pl.BlockSpec((rows, COLUMN), lambda i: (0, i))
    return pl.pallas_call(
        kernel,
        grid=(width // COLUMN,),
        in_specs=[pl.BlockSpec(mat.shape, lambda i: (0, 0))] + [wide(a.shape[0]) for a in arrays],
        out_specs=[wide(r) for r in out_rows],
        out_shape=[jax.ShapeDtypeStruct((r, width), BF16) for r in out_rows],
        compiler_params=VMEM,
        cost_estimate=pl.CostEstimate(flops=2 * mat.size * width, bytes_accessed=6 * 2**20, transcendentals=0),
    )(mat, *arrays)


def after(value, others):
    return lax.optimization_barrier((value, others))[0]


def exchange(rows, also=None):
    if also is not None:
        rows, also = lax.optimization_barrier((rows, also))
    shape = rows.shape
    got = lax.all_to_all(rows.reshape(8, shape[0] // 8, shape[1]), ("x", "core"), 0, 0, tiled=True)
    return got.reshape(shape), also


def forward_kernel(rows, w_in, w_down, out, pre, hidden):
    inner = hidden.shape[1]
    both = dot(rows[...], w_in[...])
    pre[...] = both
    hid = (silu_pieces(both[:, :inner])[0] * both[:, inner:]).astype(BF16)
    hidden[...] = hid
    out[...] = dot(hid, w_down[...]).astype(BF16)


def backward_kernel(grads, pre, w_in, w_down, far, near, d_pre):
    inner = w_down.shape[0]
    d_hidden = contract_last(grads[...], w_down[...])
    activation, slope = silu_pieces(pre[:, :inner])
    gate = (d_hidden * pre[:, inner:] * slope).astype(BF16)
    up = (d_hidden * activation).astype(BF16)
    both = jnp.concatenate([gate, up], 1)
    d_pre[...] = both
    d_rows = contract_last(both, w_in[...])
    parts = [d_rows[k : k + SLOTS] for k in range(0, d_rows.shape[0], SLOTS)]
    near[...] = jnp.concatenate([p[:NEAR] for p in parts], 0).astype(BF16)
    far[...] = jnp.concatenate([p[NEAR:] for p in parts], 0).astype(BF16)


def strips(inner, block):
    for column in range(block // 128):
        row = 0
        while row < inner:
            at = column * inner + row
            count = min(inner - row, block - at % block)
            yield column, row, at % block, at // block, count
            row += count


def grads_kernel(order, rows, grads, hidden, d_pre, *refs):
    outs, turned = refs[:-1], refs[-1]
    block, inner = rows.shape[1], hidden.shape[1]
    half = block // 2

    @pl.when(pl.program_id(0) == 0)
    def _():
        turned[...] = hidden[...].astype(F32).T.astype(BF16)

    both = contract_first(rows[...], d_pre[...]).astype(BF16)
    down = dot(turned[...], grads[...]).astype(BF16)
    for k in range(len(outs) // 2):
        top, bottom = outs[2 * k : 2 * k + 2]

        @pl.when(pl.program_id(0) == k)
        def _():
            top[:block] = both[:, :inner]
            top[block:] = both[:half, inner:]
            bottom[:half] = both[half:, inner:]
            for col, row, to_row, to_col, n in strips(inner, block):
                bottom[half + to_row : half + to_row + n, to_col * 128 : (to_col + 1) * 128] = down[
                    row : row + n, col * 128 : (col + 1) * 128
                ]


def sum_kernel(*refs):
    gate, up, down = refs[6:]
    block, inner = gate.shape[1:]
    half = block // 2
    top, bottom = total([r[...] for r in refs[:6:2]]), total([r[...] for r in refs[1:6:2]])
    gate[0] = top[:block]
    up[0, :half], up[0, half:] = top[block:], bottom[:half]
    for col, row, to_row, to_col, n in strips(inner, block):
        down[0, row : row + n, col * 128 : (col + 1) * 128] = bottom[
            half + to_row : half + to_row + n, to_col * 128 : (to_col + 1) * 128
        ]


ROW_STEPS = 2


def by_rows(kernel, arrays, weights, outs):
    rowwise = lambda rows, width: pl.BlockSpec((rows // ROW_STEPS, width), lambda i: (i, 0))
    whole = lambda shape: pl.BlockSpec(shape, lambda i: (0, 0))
    count = arrays[0].shape[0]
    return pl.pallas_call(
        kernel,
        grid=(ROW_STEPS,),
        in_specs=[rowwise(*a.shape) for a in arrays] + [whole(w.shape) for w in weights],
        out_specs=[rowwise(r, w) for r, w, _ in outs],
        out_shape=[jax.ShapeDtypeStruct((r, w), t) for r, w, t in outs],
        compiler_params=VMEM,
        cost_estimate=pl.CostEstimate(flops=6 * count * 2048 * 384, bytes_accessed=14 * 2**20, transcendentals=count * 384),
    )(*arrays, *weights)


def expert_grads(rows, grads, hidden, d_pre, hops):
    count, width = rows.shape
    inner = hidden.shape[1]
    block = width // 4
    order = (lax.axis_index("dp") + jnp.array(hops, jnp.int32)) % 4
    picked = pl.BlockSpec((count, block), lambda k, order: (0, order[k]))
    whole = lambda a: pl.BlockSpec(a.shape, lambda k, order: (0, 0))
    half = (3 * block // 2, inner)
    return pl.pallas_call(
        grads_kernel,
        grid_spec=pltpu.PrefetchScalarGridSpec(
            num_scalar_prefetch=1,
            grid=(len(hops),),
            in_specs=[picked, picked, whole(hidden), whole(d_pre)],
            out_specs=[pl.BlockSpec(half, lambda k, order: (0, 0))] * (2 * len(hops)),
            scratch_shapes=[pltpu.VMEM((inner, count), BF16)],
        ),
        out_shape=[jax.ShapeDtypeStruct(half, BF16)] * (2 * len(hops)),
        compiler_params=VMEM,
        cost_estimate=pl.CostEstimate(flops=6 * count * block * inner * len(hops), bytes_accessed=6 * 2**20, transcendentals=0),
    )(order, rows, grads, hidden, d_pre)


def sum_grads(parts, block, inner):
    shapes = [(1, block, inner), (1, block, inner), (1, inner, block)]
    return pl.pallas_call(
        sum_kernel,
        out_shape=[jax.ShapeDtypeStruct(shape, F32) for shape in shapes],
        compiler_params=VMEM,
        cost_estimate=pl.CostEstimate(flops=12 * block * inner, bytes_accessed=24 * block * inner, transcendentals=0),
    )(*parts)


def body(tokens, expert_ids, gate_numer, w_gate, w_up, w_down, shared_gate, shared_up, shared_down, d_out):
    tok_count, width = tokens.shape
    w_gate, w_up, w_down = w_gate[0], w_up[0], w_down[0]
    inner = w_gate.shape[1]
    w_in = jnp.concatenate([w_gate, w_up], 1)
    meta = jnp.concatenate([expert_ids, gate_numer], 1).astype(BF16)
    meta = jnp.pad(meta, ((0, 0), (0, META - meta.shape[1])))
    payload = jnp.concatenate([tokens, meta], 1)
    pieces = ring_gather((payload[: tok_count // 2], payload[tok_count // 2 :]))
    grads_in = [p for (p,) in ring_gather((after(d_out, pieces[-3:-1]),))]
    pieces = [p for halves in pieces for p in halves]

    rows, place, gated = select(lax.axis_index("z").reshape(1), pieces, width)
    rows, _ = exchange(after(rows, grads_in[1:3]))
    (slot_grads,) = by_columns(pick_kernel, gated, grads_in, (TARGETS * SLOTS,))
    slot_grads, rows = exchange(slot_grads, rows)

    count = rows.shape[0]
    out_rows, pre, hidden = by_rows(
        forward_kernel,
        (rows,),
        (w_in, w_down),
        ((count, width, BF16), (count, 2 * inner, F32), (count, inner, BF16)),
    )
    shared_pre_gate, shared_pre_up = dot(tokens, shared_gate), dot(tokens, shared_up)
    shared_act, shared_slope = silu_pieces(shared_pre_gate)
    shared_hidden = (shared_act * shared_pre_up).astype(BF16)
    shared_out = dot(shared_hidden, shared_down)
    shared_d_hidden = contract_last(d_out, shared_down)
    shared_d_gate = (shared_d_hidden * shared_pre_up * shared_slope).astype(BF16)
    shared_d_up = (shared_d_hidden * shared_act).astype(BF16)
    shared_d_in = contract_last(shared_d_gate, shared_gate) + contract_last(shared_d_up, shared_up)
    by_target = place.reshape(TARGETS, SLOTS, SOURCES * tok_count)
    far_mat = by_target[:, NEAR:, 2 * tok_count :].reshape(-1, 6 * tok_count).T
    near_mat = by_target[:, :NEAR, : 3 * tok_count].reshape(-1, 3 * tok_count).T
    aside = (shared_out, shared_d_in, gated.T, far_mat, near_mat)
    out_rows, (slot_grads, aside) = exchange(out_rows, (slot_grads, aside))
    shared_out, shared_d_in, out_mat, far_mat, near_mat = aside
    far_d, near_d, d_pre = by_rows(
        backward_kernel,
        (slot_grads, pre),
        (w_in, w_down),
        ((TARGETS * (SLOTS - NEAR), width, BF16), (TARGETS * NEAR, width, BF16), (count, 2 * inner, BF16)),
    )
    two_on = expert_grads(rows, slot_grads, hidden, d_pre, (2,))
    ahead_2, behind_2 = dp_step(two_on[0], 1), dp_step(two_on[1], -1)
    ahead_top, ahead_end, behind_top, behind_end, *mine = expert_grads(rows, slot_grads, hidden, d_pre, (1, 3, 0))
    blocks = (add(ahead_top, ahead_2), ahead_end, behind_top, add(behind_end, behind_2), mine)
    far_d, (out_rows, blocks) = exchange(far_d, (out_rows, blocks))
    ahead_top, ahead_end, behind_top, behind_end, mine = blocks
    ahead_end, behind_top = dp_step(ahead_end, 1), dp_step(behind_top, -1)
    ahead_top, behind_end = dp_step(ahead_top, 1), dp_step(behind_end, -1)
    near_d, far_d = exchange(near_d, far_d)

    own, a1, b1, *others = by_columns(combine_kernel, out_mat, (out_rows,), (tok_count,) * SOURCES)
    mixed, _ = ring_scatter([jnp.zeros_like(b1)] + others, (own, a1, b1))
    far_blocks = by_columns(combine_kernel, far_mat, (far_d,), (tok_count,) * 6)
    near_blocks = by_columns(combine_kernel, near_mat, (after(near_d, mixed),), (tok_count,) * 3)
    d_in, early = ring_scatter(far_blocks, near_blocks, (near_d, ahead_end, behind_top))
    parts = after([*mine, ahead_top, ahead_end, behind_top, behind_end], early)
    grad_gate, grad_up, grad_down = sum_grads(parts, width // 4, inner)

    return (
        (shared_out + total(mixed)).astype(BF16),
        (shared_d_in + total(d_in)).astype(BF16),
        grad_gate,
        grad_up,
        grad_down,
    )


def solution(mesh):
    fine = Mesh(mesh.devices.reshape(4, 4, 8, 2), ("dp", "x", "z", "core"))
    every = P(("dp", "x", "z", "core"), None)
    expert = P(("x", "z", "core"), None, None)
    return jax.shard_map(
        body,
        mesh=fine,
        in_specs=(every, every, every, expert, expert, expert, P(), P(), P(), every),
        out_specs=(
            every,
            every,
            P(("x", "z", "core"), "dp", None),
            P(("x", "z", "core"), "dp", None),
            P(("x", "z", "core"), None, "dp"),
        ),
        check_vma=False,
    )
```

```python
import jax
import jax.numpy as jnp
from jax import lax
from jax.experimental import pallas as pl
from jax.experimental.pallas import tpu as pltpu
from jax.sharding import Mesh, PartitionSpec as P

CAP = 11
GATE_SCALE = 1.0 / 64.0
F32 = jnp.float32
BF16 = jnp.bfloat16
def dot(left, right):
    return jnp.dot(left, right, preferred_element_type=F32)


def contract_last(left, right):
    return lax.dot_general(left, right, (((1,), (1,)), ((), ())), preferred_element_type=F32)


def contract_first(left, right):
    return lax.dot_general(left, right, (((0,), (0,)), ((), ())), preferred_element_type=F32)


def silu_pieces(pre_gate):
    sigmoid_val = jax.nn.sigmoid(pre_gate)
    activation = pre_gate * sigmoid_val
    return (activation, sigmoid_val + activation * (1.0 - sigmoid_val))


def ring_step(value, step):
    size = lax.axis_size("z")
    pairs = [(2 * s + c, 2 * ((s + step * (1 - 2 * c)) % size) + c) for s in range(size) for c in range(2)]
    return lax.ppermute(value, ("z", "core"), pairs)


def dp_step(value, step):
    size = lax.axis_size("dp")
    return lax.ppermute(value, "dp", [(s, (s + step) % size) for s in range(size)])


def ring_gather(parts):
    ahead = behind = parts
    pieces = [parts]
    for _ in range(3):
        hops = [(ring_step(p, 1), ring_step(q, -1)) for p, q in zip(ahead, behind)]
        ahead, behind = zip(*hops)
        pieces += [ahead, behind]
    return pieces + [tuple(ring_step(p, 1) for p in ahead)]


def add(left, right):
    return (left.astype(F32) + right.astype(F32)).astype(BF16)


def ring_scatter(far, near, before_third=()):
    b1, a2, b2, a3, b3, a4 = far
    own, a1, b1_too = near
    ahead, behind = add(ring_step(a4, -1), a3), b3
    ahead, behind = add(ring_step(ahead, -1), a2), add(ring_step(behind, 1), b2)
    ahead = after(ahead, before_third)
    ahead, behind = add(ring_step(ahead, -1), a1), total((ring_step(behind, 1), b1, b1_too)).astype(BF16)
    return (ring_step(ahead, -1), ring_step(behind, 1), own), (ahead, behind)


def total(terms):
    return sum(t.astype(F32) for t in terms)


SOURCES = 8
TARGETS = 8
SLOTS = SOURCES * CAP
NEAR = 32
META = 128


def select_kernel(z, *refs):
    count = (len(refs) - 3) // 2
    pieces, metas = refs[:count], refs[count : 2 * count]
    rows, place, gated = refs[2 * count :]
    cols = place.shape[1]
    toks = cols // SOURCES

    @pl.when(pl.program_id(0) == 0)
    def _():
        meta = jnp.concatenate([m[...] for m in metas], 0).astype(F32).T
        ids, gates = meta[:8], meta[8:16] * GATE_SCALE
        lane = lax.broadcasted_iota(jnp.int32, (cols, cols), 1)
        sub = lax.broadcasted_iota(jnp.int32, (cols, cols), 0)
        before = jnp.where((sub < lane) & (sub >= (lane // toks) * toks), 1.0, 0.0).astype(BF16)
        member, gate = [], []
        for k in range(TARGETS):
            match = ids == ((k // 2) * 16 + 2 * z[0] + k % 2).astype(F32)
            member.append(jnp.max(jnp.where(match, 1.0, 0.0), 0, keepdims=True))
            gate.append(jnp.sum(jnp.where(match, gates, 0.0), 0, keepdims=True))
        member = jnp.concatenate(member, 0)
        rank = dot(member.astype(BF16), before)
        first = (lax.broadcasted_iota(jnp.int32, member.shape, 1) // toks * CAP).astype(F32)
        code = jnp.where(member > 0.0, rank + first, -1.0)
        slot = lax.broadcasted_iota(jnp.int32, (SLOTS, cols), 0).astype(F32)
        hits = [code[k : k + 1] == slot for k in range(TARGETS)]
        place[...] = jnp.concatenate([jnp.where(h, 1.0, 0.0) for h in hits], 0).astype(BF16)
        gated[...] = jnp.concatenate([jnp.where(h, g, 0.0) for h, g in zip(hits, gate)], 0).astype(BF16)

    rows[...] = dot(place[...], jnp.concatenate([p[...] for p in pieces], 0)).astype(BF16)


def pick_kernel(mat, *refs):
    refs[-1][...] = dot(mat[...], jnp.concatenate([p[...] for p in refs[:-1]], 0)).astype(BF16)


def combine_kernel(mat, rows, *outs):
    summed = dot(mat[...], rows[...]).astype(BF16)
    toks = outs[0].shape[0]
    for i, out in enumerate(outs):
        out[...] = summed[i * toks : (i + 1) * toks]


VMEM = pltpu.CompilerParams(vmem_limit_bytes=60 * 2**20)
COLUMN = 1024


def select(z, pieces, width):
    part, count = pieces[0].shape[0], len(pieces)
    cols = part * count
    whole = pl.BlockSpec((TARGETS * SLOTS, cols), lambda i, z: (0, 0))
    wide = lambda rows: pl.BlockSpec((rows, COLUMN), lambda i, z: (0, i))
    return pl.pallas_call(
        select_kernel,
        grid_spec=pltpu.PrefetchScalarGridSpec(
            num_scalar_prefetch=1,
            grid=(width // COLUMN,),
            in_specs=[wide(part)] * count + [pl.BlockSpec((part, META), lambda i, z: (0, width // META))] * count,
            out_specs=[wide(TARGETS * SLOTS), whole, whole],
        ),
        out_shape=[jax.ShapeDtypeStruct((TARGETS * SLOTS, w), BF16) for w in (width, cols, cols)],
        compiler_params=VMEM,
        cost_estimate=pl.CostEstimate(flops=2 * TARGETS * SLOTS * cols * width, bytes_accessed=8 * 2**20, transcendentals=0),
    )(z, *pieces, *pieces)


def by_columns(kernel, mat, arrays, out_rows):
    width = arrays[0].shape[1]
    wide = lambda rows: pl.BlockSpec((rows, COLUMN), lambda i: (0, i))
    return pl.pallas_call(
        kernel,
        grid=(width // COLUMN,),
        in_specs=[pl.BlockSpec(mat.shape, lambda i: (0, 0))] + [wide(a.shape[0]) for a in arrays],
        out_specs=[wide(r) for r in out_rows],
        out_shape=[jax.ShapeDtypeStruct((r, width), BF16) for r in out_rows],
        compiler_params=VMEM,
        cost_estimate=pl.CostEstimate(flops=2 * mat.size * width, bytes_accessed=6 * 2**20, transcendentals=0),
    )(mat, *arrays)


def after(value, others):
    return lax.optimization_barrier((value, others))[0]


def exchange(rows, also=None):
    if also is not None:
        rows, also = lax.optimization_barrier((rows, also))
    shape = rows.shape
    got = lax.all_to_all(rows.reshape(8, shape[0] // 8, shape[1]), ("x", "core"), 0, 0, tiled=True)
    return got.reshape(shape), also


def forward_kernel(rows, w_in, w_down, out, pre, hidden):
    inner = hidden.shape[1]
    both = dot(rows[...], w_in[...])
    pre[...] = both
    hid = (silu_pieces(both[:, :inner])[0] * both[:, inner:]).astype(BF16)
    hidden[...] = hid
    out[...] = dot(hid, w_down[...]).astype(BF16)


def backward_kernel(grads, pre, w_in, w_down, far, near, d_pre):
    inner = w_down.shape[0]
    d_hidden = contract_last(grads[...], w_down[...])
    activation, slope = silu_pieces(pre[:, :inner])
    gate = (d_hidden * pre[:, inner:] * slope).astype(BF16)
    up = (d_hidden * activation).astype(BF16)
    both = jnp.concatenate([gate, up], 1)
    d_pre[...] = both
    d_rows = contract_last(both, w_in[...])
    parts = [d_rows[k : k + SLOTS] for k in range(0, d_rows.shape[0], SLOTS)]
    near[...] = jnp.concatenate([p[:NEAR] for p in parts], 0).astype(BF16)
    far[...] = jnp.concatenate([p[NEAR:] for p in parts], 0).astype(BF16)


def strips(inner, block):
    for column in range(block // 128):
        row = 0
        while row < inner:
            at = column * inner + row
            count = min(inner - row, block - at % block)
            yield column, row, at % block, at // block, count
            row += count


def grads_kernel(order, rows, grads, hidden, d_pre, *refs):
    outs, turned = refs[:-1], refs[-1]
    block, inner = rows.shape[1], hidden.shape[1]
    half = block // 2

    @pl.when(pl.program_id(0) == 0)
    def _():
        turned[...] = hidden[...].astype(F32).T.astype(BF16)

    both = contract_first(rows[...], d_pre[...]).astype(BF16)
    down = dot(turned[...], grads[...]).astype(BF16)
    for k in range(len(outs) // 2):
        top, bottom = outs[2 * k : 2 * k + 2]

        @pl.when(pl.program_id(0) == k)
        def _():
            top[:block] = both[:, :inner]
            top[block:] = both[:half, inner:]
            bottom[:half] = both[half:, inner:]
            for col, row, to_row, to_col, n in strips(inner, block):
                bottom[half + to_row : half + to_row + n, to_col * 128 : (to_col + 1) * 128] = down[
                    row : row + n, col * 128 : (col + 1) * 128
                ]


def sum_kernel(*refs):
    gate, up, down = refs[6:]
    block, inner = gate.shape[1:]
    half = block // 2
    top, bottom = total([r[...] for r in refs[:6:2]]), total([r[...] for r in refs[1:6:2]])
    gate[0] = top[:block]
    up[0, :half], up[0, half:] = top[block:], bottom[:half]
    for col, row, to_row, to_col, n in strips(inner, block):
        down[0, row : row + n, col * 128 : (col + 1) * 128] = bottom[
            half + to_row : half + to_row + n, to_col * 128 : (to_col + 1) * 128
        ]


ROW_STEPS = 2


def by_rows(kernel, arrays, weights, outs):
    rowwise = lambda rows, width: pl.BlockSpec((rows // ROW_STEPS, width), lambda i: (i, 0))
    whole = lambda shape: pl.BlockSpec(shape, lambda i: (0, 0))
    count = arrays[0].shape[0]
    return pl.pallas_call(
        kernel,
        grid=(ROW_STEPS,),
        in_specs=[rowwise(*a.shape) for a in arrays] + [whole(w.shape) for w in weights],
        out_specs=[rowwise(r, w) for r, w, _ in outs],
        out_shape=[jax.ShapeDtypeStruct((r, w), t) for r, w, t in outs],
        compiler_params=VMEM,
        cost_estimate=pl.CostEstimate(flops=6 * count * 2048 * 384, bytes_accessed=14 * 2**20, transcendentals=count * 384),
    )(*arrays, *weights)


def expert_grads(rows, grads, hidden, d_pre, hops):
    count, width = rows.shape
    inner = hidden.shape[1]
    block = width // 4
    order = (lax.axis_index("dp") + jnp.array(hops, jnp.int32)) % 4
    picked = pl.BlockSpec((count, block), lambda k, order: (0, order[k]))
    whole = lambda a: pl.BlockSpec(a.shape, lambda k, order: (0, 0))
    half = (3 * block // 2, inner)
    return pl.pallas_call(
        grads_kernel,
        grid_spec=pltpu.PrefetchScalarGridSpec(
            num_scalar_prefetch=1,
            grid=(len(hops),),
            in_specs=[picked, picked, whole(hidden), whole(d_pre)],
            out_specs=[pl.BlockSpec(half, lambda k, order: (0, 0))] * (2 * len(hops)),
            scratch_shapes=[pltpu.VMEM((inner, count), BF16)],
        ),
        out_shape=[jax.ShapeDtypeStruct(half, BF16)] * (2 * len(hops)),
        compiler_params=VMEM,
        cost_estimate=pl.CostEstimate(flops=6 * count * block * inner * len(hops), bytes_accessed=6 * 2**20, transcendentals=0),
    )(order, rows, grads, hidden, d_pre)


def sum_grads(parts, block, inner):
    shapes = [(1, block, inner), (1, block, inner), (1, inner, block)]
    return pl.pallas_call(
        sum_kernel,
        out_shape=[jax.ShapeDtypeStruct(shape, F32) for shape in shapes],
        compiler_params=VMEM,
        cost_estimate=pl.CostEstimate(flops=12 * block * inner, bytes_accessed=24 * block * inner, transcendentals=0),
    )(*parts)


def body(tokens, expert_ids, gate_numer, w_gate, w_up, w_down, shared_gate, shared_up, shared_down, d_out):
    tok_count, width = tokens.shape
    w_gate, w_up, w_down = w_gate[0], w_up[0], w_down[0]
    inner = w_gate.shape[1]
    w_in = jnp.concatenate([w_gate, w_up], 1)
    meta = jnp.concatenate([expert_ids, gate_numer], 1).astype(BF16)
    meta = jnp.pad(meta, ((0, 0), (0, META - meta.shape[1])))
    payload = jnp.concatenate([tokens, meta], 1)
    pieces = ring_gather((payload[: tok_count // 2], payload[tok_count // 2 :]))
    grads_in = [p for (p,) in ring_gather((after(d_out, pieces[-3:-1]),))]
    pieces = [p for halves in pieces for p in halves]

    rows, place, gated = select(lax.axis_index("z").reshape(1), pieces, width)
    rows, _ = exchange(after(rows, grads_in[1:3]))
    (slot_grads,) = by_columns(pick_kernel, gated, grads_in, (TARGETS * SLOTS,))
    slot_grads, rows = exchange(slot_grads, rows)

    count = rows.shape[0]
    out_rows, pre, hidden = by_rows(
        forward_kernel,
        (rows,),
        (w_in, w_down),
        ((count, width, BF16), (count, 2 * inner, F32), (count, inner, BF16)),
    )
    shared_pre_gate, shared_pre_up = dot(tokens, shared_gate), dot(tokens, shared_up)
    shared_act, shared_slope = silu_pieces(shared_pre_gate)
    shared_hidden = (shared_act * shared_pre_up).astype(BF16)
    shared_out = dot(shared_hidden, shared_down)
    shared_d_hidden = contract_last(d_out, shared_down)
    shared_d_gate = (shared_d_hidden * shared_pre_up * shared_slope).astype(BF16)
    shared_d_up = (shared_d_hidden * shared_act).astype(BF16)
    shared_d_in = contract_last(shared_d_gate, shared_gate) + contract_last(shared_d_up, shared_up)
    by_target = place.reshape(TARGETS, SLOTS, SOURCES * tok_count)
    far_mat = by_target[:, NEAR:, 2 * tok_count :].reshape(-1, 6 * tok_count).T
    near_mat = by_target[:, :NEAR, : 3 * tok_count].reshape(-1, 3 * tok_count).T
    aside = (shared_out, shared_d_in, gated.T, far_mat, near_mat)
    out_rows, (slot_grads, aside) = exchange(out_rows, (slot_grads, aside))
    shared_out, shared_d_in, out_mat, far_mat, near_mat = aside
    far_d, near_d, d_pre = by_rows(
        backward_kernel,
        (slot_grads, pre),
        (w_in, w_down),
        ((TARGETS * (SLOTS - NEAR), width, BF16), (TARGETS * NEAR, width, BF16), (count, 2 * inner, BF16)),
    )
    two_on = expert_grads(rows, slot_grads, hidden, d_pre, (2,))
    ahead_2, behind_2 = dp_step(two_on[0], 1), dp_step(two_on[1], -1)
    ahead_top, ahead_end, behind_top, behind_end, *mine = expert_grads(rows, slot_grads, hidden, d_pre, (1, 3, 0))
    blocks = (add(ahead_top, ahead_2), ahead_end, behind_top, add(behind_end, behind_2), mine)
    far_d, (out_rows, blocks) = exchange(far_d, (out_rows, blocks))
    ahead_top, ahead_end, behind_top, behind_end, mine = blocks
    ahead_end, behind_top = dp_step(ahead_end, 1), dp_step(behind_top, -1)
    ahead_top, behind_end = dp_step(ahead_top, 1), dp_step(behind_end, -1)
    near_d, far_d = exchange(near_d, far_d)

    own, a1, b1, *others = by_columns(combine_kernel, out_mat, (out_rows,), (tok_count,) * SOURCES)
    mixed, _ = ring_scatter([jnp.zeros_like(b1)] + others, (own, a1, b1))
    far_blocks = by_columns(combine_kernel, far_mat, (far_d,), (tok_count,) * 6)
    near_blocks = by_columns(combine_kernel, near_mat, (after(near_d, mixed),), (tok_count,) * 3)
    d_in, early = ring_scatter(far_blocks, near_blocks, (near_d, ahead_end, behind_top))
    parts = after([*mine, ahead_top, ahead_end, behind_top, behind_end], early)
    grad_gate, grad_up, grad_down = sum_grads(parts, width // 4, inner)

    return (
        (shared_out + total(mixed)).astype(BF16),
        (shared_d_in + total(d_in)).astype(BF16),
        grad_gate,
        grad_up,
        grad_down,
    )


def solution(mesh):
    fine = Mesh(mesh.devices.reshape(4, 4, 8, 2), ("dp", "x", "z", "core"))
    every = P(("dp", "x", "z", "core"), None)
    expert = P(("x", "z", "core"), None, None)
    return jax.shard_map(
        body,
        mesh=fine,
        in_specs=(every, every, every, expert, expert, expert, P(), P(), P(), every),
        out_specs=(
            every,
            every,
            P(("x", "z", "core"), "dp", None),
            P(("x", "z", "core"), "dp", None),
            P(("x", "z", "core"), None, "dp"),
        ),
        check_vma=False,
    )
```

```python
import jax
import jax.numpy as jnp
from jax import lax
from jax.experimental import pallas as pl
from jax.experimental.pallas import tpu as pltpu
from jax.sharding import Mesh, PartitionSpec as P

CAP = 11
GATE_SCALE = 1.0 / 64.0
F32 = jnp.float32
BF16 = jnp.bfloat16
def dot(left, right):
    return jnp.dot(left, right, preferred_element_type=F32)


def contract_last(left, right):
    return lax.dot_general(left, right, (((1,), (1,)), ((), ())), preferred_element_type=F32)


def contract_first(left, right):
    return lax.dot_general(left, right, (((0,), (0,)), ((), ())), preferred_element_type=F32)


def silu_pieces(pre_gate):
    sigmoid_val = jax.nn.sigmoid(pre_gate)
    activation = pre_gate * sigmoid_val
    return (activation, sigmoid_val + activation * (1.0 - sigmoid_val))


def ring_step(value, step):
    size = lax.axis_size("z")
    pairs = [(2 * s + c, 2 * ((s + step * (1 - 2 * c)) % size) + c) for s in range(size) for c in range(2)]
    return lax.ppermute(value, ("z", "core"), pairs)


def dp_step(value, step):
    size = lax.axis_size("dp")
    return lax.ppermute(value, "dp", [(s, (s + step) % size) for s in range(size)])


def ring_gather(parts):
    ahead = behind = parts
    pieces = [parts]
    for _ in range(3):
        hops = [(ring_step(p, 1), ring_step(q, -1)) for p, q in zip(ahead, behind)]
        ahead, behind = zip(*hops)
        pieces += [ahead, behind]
    return pieces + [tuple(ring_step(p, 1) for p in ahead)]


def add(left, right):
    return (left.astype(F32) + right.astype(F32)).astype(BF16)


def ring_scatter(far, near, before_third=()):
    b1, a2, b2, a3, b3, a4 = far
    own, a1, b1_too = near
    ahead, behind = add(ring_step(a4, -1), a3), b3
    ahead, behind = add(ring_step(ahead, -1), a2), add(ring_step(behind, 1), b2)
    ahead = after(ahead, before_third)
    ahead, behind = add(ring_step(ahead, -1), a1), total((ring_step(behind, 1), b1, b1_too)).astype(BF16)
    return (ring_step(ahead, -1), ring_step(behind, 1), own), (ahead, behind)


def total(terms):
    return sum(t.astype(F32) for t in terms)


SOURCES = 8
TARGETS = 8
SLOTS = SOURCES * CAP
NEAR = 32
META = 128


def select_kernel(z, *refs):
    count = (len(refs) - 3) // 2
    pieces, metas = refs[:count], refs[count : 2 * count]
    rows, place, gated = refs[2 * count :]
    cols = place.shape[1]
    toks = cols // SOURCES

    @pl.when(pl.program_id(0) == 0)
    def _():
        meta = jnp.concatenate([m[...] for m in metas], 0).astype(F32).T
        ids, gates = meta[:8], meta[8:16] * GATE_SCALE
        lane = lax.broadcasted_iota(jnp.int32, (cols, cols), 1)
        sub = lax.broadcasted_iota(jnp.int32, (cols, cols), 0)
        before = jnp.where((sub < lane) & (sub >= (lane // toks) * toks), 1.0, 0.0).astype(BF16)
        member, gate = [], []
        for k in range(TARGETS):
            match = ids == ((k // 2) * 16 + 2 * z[0] + k % 2).astype(F32)
            member.append(jnp.max(jnp.where(match, 1.0, 0.0), 0, keepdims=True))
            gate.append(jnp.sum(jnp.where(match, gates, 0.0), 0, keepdims=True))
        member = jnp.concatenate(member, 0)
        rank = dot(member.astype(BF16), before)
        first = (lax.broadcasted_iota(jnp.int32, member.shape, 1) // toks * CAP).astype(F32)
        code = jnp.where(member > 0.0, rank + first, -1.0)
        slot = lax.broadcasted_iota(jnp.int32, (SLOTS, cols), 0).astype(F32)
        hits = [code[k : k + 1] == slot for k in range(TARGETS)]
        place[...] = jnp.concatenate([jnp.where(h, 1.0, 0.0) for h in hits], 0).astype(BF16)
        gated[...] = jnp.concatenate([jnp.where(h, g, 0.0) for h, g in zip(hits, gate)], 0).astype(BF16)

    rows[...] = dot(place[...], jnp.concatenate([p[...] for p in pieces], 0)).astype(BF16)


def pick_kernel(mat, *refs):
    refs[-1][...] = dot(mat[...], jnp.concatenate([p[...] for p in refs[:-1]], 0)).astype(BF16)


def combine_kernel(mat, rows, *outs):
    summed = dot(mat[...], rows[...]).astype(BF16)
    toks = outs[0].shape[0]
    for i, out in enumerate(outs):
        out[...] = summed[i * toks : (i + 1) * toks]


VMEM = pltpu.CompilerParams(vmem_limit_bytes=60 * 2**20)
COLUMN = 1024


def select(z, pieces, width):
    part, count = pieces[0].shape[0], len(pieces)
    cols = part * count
    whole = pl.BlockSpec((TARGETS * SLOTS, cols), lambda i, z: (0, 0))
    wide = lambda rows: pl.BlockSpec((rows, COLUMN), lambda i, z: (0, i))
    return pl.pallas_call(
        select_kernel,
        grid_spec=pltpu.PrefetchScalarGridSpec(
            num_scalar_prefetch=1,
            grid=(width // COLUMN,),
            in_specs=[wide(part)] * count + [pl.BlockSpec((part, META), lambda i, z: (0, width // META))] * count,
            out_specs=[wide(TARGETS * SLOTS), whole, whole],
        ),
        out_shape=[jax.ShapeDtypeStruct((TARGETS * SLOTS, w), BF16) for w in (width, cols, cols)],
        compiler_params=VMEM,
        cost_estimate=pl.CostEstimate(flops=2 * TARGETS * SLOTS * cols * width, bytes_accessed=8 * 2**20, transcendentals=0),
    )(z, *pieces, *pieces)


def by_columns(kernel, mat, arrays, out_rows):
    width = arrays[0].shape[1]
    wide = lambda rows: pl.BlockSpec((rows, COLUMN), lambda i: (0, i))
    return pl.pallas_call(
        kernel,
        grid=(width // COLUMN,),
        in_specs=[pl.BlockSpec(mat.shape, lambda i: (0, 0))] + [wide(a.shape[0]) for a in arrays],
        out_specs=[wide(r) for r in out_rows],
        out_shape=[jax.ShapeDtypeStruct((r, width), BF16) for r in out_rows],
        compiler_params=VMEM,
        cost_estimate=pl.CostEstimate(flops=2 * mat.size * width, bytes_accessed=6 * 2**20, transcendentals=0),
    )(mat, *arrays)


def after(value, others):
    return lax.optimization_barrier((value, others))[0]


def exchange(rows, also=None):
    if also is not None:
        rows, also = lax.optimization_barrier((rows, also))
    shape = rows.shape
    got = lax.all_to_all(rows.reshape(8, shape[0] // 8, shape[1]), ("x", "core"), 0, 0, tiled=True)
    return got.reshape(shape), also


def forward_kernel(rows, w_in, w_down, out, pre, hidden):
    inner = hidden.shape[1]
    both = dot(rows[...], w_in[...])
    pre[...] = both
    hid = (silu_pieces(both[:, :inner])[0] * both[:, inner:]).astype(BF16)
    hidden[...] = hid
    out[...] = dot(hid, w_down[...]).astype(BF16)


def backward_kernel(grads, pre, w_in, w_down, far, near, d_pre):
    inner = w_down.shape[0]
    d_hidden = contract_last(grads[...], w_down[...])
    activation, slope = silu_pieces(pre[:, :inner])
    gate = (d_hidden * pre[:, inner:] * slope).astype(BF16)
    up = (d_hidden * activation).astype(BF16)
    both = jnp.concatenate([gate, up], 1)
    d_pre[...] = both
    d_rows = contract_last(both, w_in[...])
    parts = [d_rows[k : k + SLOTS] for k in range(0, d_rows.shape[0], SLOTS)]
    near[...] = jnp.concatenate([p[:NEAR] for p in parts], 0).astype(BF16)
    far[...] = jnp.concatenate([p[NEAR:] for p in parts], 0).astype(BF16)


def strips(inner, block):
    for column in range(block // 128):
        row = 0
        while row < inner:
            at = column * inner + row
            count = min(inner - row, block - at % block)
            yield column, row, at % block, at // block, count
            row += count


def grads_kernel(order, rows, grads, hidden, d_pre, *refs):
    outs, turned = refs[:-1], refs[-1]
    block, inner = rows.shape[1], hidden.shape[1]
    half = block // 2

    @pl.when(pl.program_id(0) == 0)
    def _():
        turned[...] = hidden[...].astype(F32).T.astype(BF16)

    both = contract_first(rows[...], d_pre[...]).astype(BF16)
    down = dot(turned[...], grads[...]).astype(BF16)
    for k in range(len(outs) // 2):
        top, bottom = outs[2 * k : 2 * k + 2]

        @pl.when(pl.program_id(0) == k)
        def _():
            top[:block] = both[:, :inner]
            top[block:] = both[:half, inner:]
            bottom[:half] = both[half:, inner:]
            for col, row, to_row, to_col, n in strips(inner, block):
                bottom[half + to_row : half + to_row + n, to_col * 128 : (to_col + 1) * 128] = down[
                    row : row + n, col * 128 : (col + 1) * 128
                ]


def sum_kernel(*refs):
    gate, up, down = refs[6:]
    block, inner = gate.shape[1:]
    half = block // 2
    top, bottom = total([r[...] for r in refs[:6:2]]), total([r[...] for r in refs[1:6:2]])
    gate[0] = top[:block]
    up[0, :half], up[0, half:] = top[block:], bottom[:half]
    for col, row, to_row, to_col, n in strips(inner, block):
        down[0, row : row + n, col * 128 : (col + 1) * 128] = bottom[
            half + to_row : half + to_row + n, to_col * 128 : (to_col + 1) * 128
        ]


ROW_STEPS = 2


def by_rows(kernel, arrays, weights, outs):
    rowwise = lambda rows, width: pl.BlockSpec((rows // ROW_STEPS, width), lambda i: (i, 0))
    whole = lambda shape: pl.BlockSpec(shape, lambda i: (0, 0))
    count = arrays[0].shape[0]
    return pl.pallas_call(
        kernel,
        grid=(ROW_STEPS,),
        in_specs=[rowwise(*a.shape) for a in arrays] + [whole(w.shape) for w in weights],
        out_specs=[rowwise(r, w) for r, w, _ in outs],
        out_shape=[jax.ShapeDtypeStruct((r, w), t) for r, w, t in outs],
        compiler_params=VMEM,
        cost_estimate=pl.CostEstimate(flops=6 * count * 2048 * 384, bytes_accessed=14 * 2**20, transcendentals=count * 384),
    )(*arrays, *weights)


def expert_grads(rows, grads, hidden, d_pre, hops):
    count, width = rows.shape
    inner = hidden.shape[1]
    block = width // 4
    order = (lax.axis_index("dp") + jnp.array(hops, jnp.int32)) % 4
    picked = pl.BlockSpec((count, block), lambda k, order: (0, order[k]))
    whole = lambda a: pl.BlockSpec(a.shape, lambda k, order: (0, 0))
    half = (3 * block // 2, inner)
    return pl.pallas_call(
        grads_kernel,
        grid_spec=pltpu.PrefetchScalarGridSpec(
            num_scalar_prefetch=1,
            grid=(len(hops),),
            in_specs=[picked, picked, whole(hidden), whole(d_pre)],
            out_specs=[pl.BlockSpec(half, lambda k, order: (0, 0))] * (2 * len(hops)),
            scratch_shapes=[pltpu.VMEM((inner, count), BF16)],
        ),
        out_shape=[jax.ShapeDtypeStruct(half, BF16)] * (2 * len(hops)),
        compiler_params=VMEM,
        cost_estimate=pl.CostEstimate(flops=6 * count * block * inner * len(hops), bytes_accessed=6 * 2**20, transcendentals=0),
    )(order, rows, grads, hidden, d_pre)


def sum_grads(parts, block, inner):
    shapes = [(1, block, inner), (1, block, inner), (1, inner, block)]
    return pl.pallas_call(
        sum_kernel,
        out_shape=[jax.ShapeDtypeStruct(shape, F32) for shape in shapes],
        compiler_params=VMEM,
        cost_estimate=pl.CostEstimate(flops=12 * block * inner, bytes_accessed=24 * block * inner, transcendentals=0),
    )(*parts)


def body(tokens, expert_ids, gate_numer, w_gate, w_up, w_down, shared_gate, shared_up, shared_down, d_out):
    tok_count, width = tokens.shape
    w_gate, w_up, w_down = w_gate[0], w_up[0], w_down[0]
    inner = w_gate.shape[1]
    w_in = jnp.concatenate([w_gate, w_up], 1)
    meta = jnp.concatenate([expert_ids, gate_numer], 1).astype(BF16)
    meta = jnp.pad(meta, ((0, 0), (0, META - meta.shape[1])))
    payload = jnp.concatenate([tokens, meta], 1)
    pieces = ring_gather((payload[: tok_count // 2], payload[tok_count // 2 :]))
    grads_in = [p for (p,) in ring_gather((after(d_out, pieces[-3:-1]),))]
    pieces = [p for halves in pieces for p in halves]

    rows, place, gated = select(lax.axis_index("z").reshape(1), pieces, width)
    rows, _ = exchange(after(rows, grads_in[1:3]))
    (slot_grads,) = by_columns(pick_kernel, gated, grads_in, (TARGETS * SLOTS,))
    slot_grads, rows = exchange(slot_grads, rows)

    count = rows.shape[0]
    out_rows, pre, hidden = by_rows(
        forward_kernel,
        (rows,),
        (w_in, w_down),
        ((count, width, BF16), (count, 2 * inner, F32), (count, inner, BF16)),
    )
    shared_pre_gate, shared_pre_up = dot(tokens, shared_gate), dot(tokens, shared_up)
    shared_act, shared_slope = silu_pieces(shared_pre_gate)
    shared_hidden = (shared_act * shared_pre_up).astype(BF16)
    shared_out = dot(shared_hidden, shared_down)
    shared_d_hidden = contract_last(d_out, shared_down)
    shared_d_gate = (shared_d_hidden * shared_pre_up * shared_slope).astype(BF16)
    shared_d_up = (shared_d_hidden * shared_act).astype(BF16)
    shared_d_in = contract_last(shared_d_gate, shared_gate) + contract_last(shared_d_up, shared_up)
    by_target = place.reshape(TARGETS, SLOTS, SOURCES * tok_count)
    far_mat = by_target[:, NEAR:, 2 * tok_count :].reshape(-1, 6 * tok_count).T
    near_mat = by_target[:, :NEAR, : 3 * tok_count].reshape(-1, 3 * tok_count).T
    last = (SOURCES - 1) * tok_count
    out_mats = (gated[:, last:].T, gated[:, :last].T)
    aside = (shared_out, shared_d_in, out_mats, far_mat, near_mat)
    out_rows, (slot_grads, aside) = exchange(out_rows, (slot_grads, aside))
    shared_out, shared_d_in, out_mats, far_mat, near_mat = aside
    far_d, near_d, d_pre = by_rows(
        backward_kernel,
        (slot_grads, pre),
        (w_in, w_down),
        ((TARGETS * (SLOTS - NEAR), width, BF16), (TARGETS * NEAR, width, BF16), (count, 2 * inner, BF16)),
    )
    two_on = expert_grads(rows, slot_grads, hidden, d_pre, (2,))
    ahead_2, behind_2 = dp_step(two_on[0], 1), dp_step(two_on[1], -1)
    ahead_top, ahead_end, behind_top, behind_end, *mine = expert_grads(rows, slot_grads, hidden, d_pre, (1, 3, 0))
    blocks = (add(ahead_top, ahead_2), ahead_end, behind_top, add(behind_end, behind_2), mine)
    far_d, (out_rows, blocks) = exchange(far_d, (out_rows, blocks))
    ahead_top, ahead_end, behind_top, behind_end, mine = blocks
    ahead_end, behind_top = dp_step(ahead_end, 1), dp_step(behind_top, -1)
    ahead_top, behind_end = dp_step(ahead_top, 1), dp_step(behind_end, -1)
    near_d, far_d = exchange(near_d, far_d)

    (a4,) = by_columns(combine_kernel, out_mats[0], (out_rows,), (tok_count,))
    own, a1, b1, *others = by_columns(combine_kernel, out_mats[1], (out_rows,), (tok_count,) * (SOURCES - 1))
    others = others + [a4]
    mixed, _ = ring_scatter([jnp.zeros_like(b1)] + others, (own, a1, b1))
    far_blocks = by_columns(combine_kernel, far_mat, (far_d,), (tok_count,) * 6)
    near_blocks = by_columns(combine_kernel, near_mat, (after(near_d, mixed),), (tok_count,) * 3)
    d_in, early = ring_scatter(far_blocks, near_blocks, (near_d, ahead_end, behind_top))
    parts = after([*mine, ahead_top, ahead_end, behind_top, behind_end], early)
    grad_gate, grad_up, grad_down = sum_grads(parts, width // 4, inner)

    return (
        (shared_out + total(mixed)).astype(BF16),
        (shared_d_in + total(d_in)).astype(BF16),
        grad_gate,
        grad_up,
        grad_down,
    )


def solution(mesh):
    fine = Mesh(mesh.devices.reshape(4, 4, 8, 2), ("dp", "x", "z", "core"))
    every = P(("dp", "x", "z", "core"), None)
    expert = P(("x", "z", "core"), None, None)
    return jax.shard_map(
        body,
        mesh=fine,
        in_specs=(every, every, every, expert, expert, expert, P(), P(), P(), every),
        out_specs=(
            every,
            every,
            P(("x", "z", "core"), "dp", None),
            P(("x", "z", "core"), "dp", None),
            P(("x", "z", "core"), None, "dp"),
        ),
        check_vma=False,
    )
```
